32 devices in a mesh: group: 2 (over y), latent: 16 (over z, x, core).
Axes of the slice: x: 2, y: 2, z: 4, core: 2. Of those that a mesh axis runs over, the one named last changes fastest.
Arguments:
- activations: bfloat16 [16, 256, 7168], P('group', 'latent'), parts along dimension 0, may hold values from -6 to 6
- enc_weight: bfloat16 [32, 7168, 128], P(('group', 'latent')), parts along dimension 0, may hold values from -0.0625 to 0.0625
- enc_bias: float32 [32, 128], P(('group', 'latent')), parts along dimension 0, may hold values from -3 to 3
- dec_weight: bfloat16 [32, 128, 7168], P(('group', 'latent')), parts along dimension 0, may hold values from -0.5 to 0.5
- dec_bias: float32 [14336], P('group'), parts along dimension 0, may hold values from -3 to 3
- active: int32 [16, 3], P('group'), parts along dimension 0, may hold values from 0 to 15, all different within a row; in each aligned block of 8 rows (0 to 7, 8 to 15, ...) at most 2 rows name the same one
Outputs:
- enc_grad: float32 [32, 7168, 128], P(('group', 'latent')), parts along dimension 0
- enc_bias_grad: float32 [32, 128], P(('group', 'latent')), parts along dimension 0
- dec_grad: float32 [32, 128, 7168], P(('group', 'latent')), parts along dimension 0
- dec_bias_grad: float32 [14336], P('group'), parts along dimension 0
The draws below stay inside these ranges and needn't reach their ends.
There are 2 independent parts, one for each index of `group`. The reference program is written for one: setup_inputs(seed, part) draws one part's arguments, and reference() takes and returns one part's arrays. A program takes and returns all parts, laid end to end along the dimension named above; each array names one. Nothing has to cross between parts.
Inputs may be any that keep to these rules, and one draw needn't show every extreme that they name: `active`: each row names 3 different blocks; no block is named by more than 2 rows, and some block by exactly 2.
All inputs are finite; a program needn't handle non-finite values.
Results may differ from the reference program's by a relative error of at most 0.0045.
Values may be sent and summed in bfloat16 or wider, within the bound.
No kernel may reach another device: no remote copies, remote signals or barrier semaphores. Data moves between devices by JAX's collectives and lax.ppermute only.
A program may use at most 128 MiB of HBM per device.

```python
import math
import jax
import jax.numpy as jnp
import numpy as np
from jax import lax

D = 3584
BW = 128
K = 3
SPAN = 256
MOST = 2
BLOCKS = 16
SPANS = 8


def level_of(rng, shape, shards, smallest, top_value):
    level, own = 1.0, jax.random.fold_in(rng, 6)
    for dim, parts in shards:
        steps = jnp.exp(jax.random.uniform(jax.random.fold_in(own, dim), (parts,), jnp.float32, smallest / len(shards), top_value / len(shards)))
        level = level * jnp.repeat(steps, shape[dim] // parts).reshape([-1 if axis == dim else 1 for axis in range(len(shape))])
    return level


def deal_out(own_key, own, number, rows, number_of, top, reach, lean):
    sequence = jax.random.permutation(own_key, number_of)
    crowded, common = load_shares(number_of, rows * top, reach, lean, True), load_shares(number_of, rows * top, reach, lean, False)
    places = jnp.arange(number_of)

    def named(lengths, offset_by):
        used = int((lengths > 0).sum())
        fixed = max(1, used // 4)
        passed = fixed + (places - fixed + offset_by * (used - fixed)) % max(1, number_of - fixed)
        return jnp.zeros((number_of,), jnp.int32).at[sequence[jnp.where(places < fixed, places, passed)]].set(jnp.asarray(lengths, jnp.int32))

    lengths = jnp.where(number % 4 == 0, named(crowded, number // 4), named(common, number - number // 4 - 1))
    mixed = jax.random.permutation(jax.random.fold_in(own, 3), number_of)
    source_of, taker = mixed[0:number_of // 2 * 2:2], mixed[1:number_of // 2 * 2:2]
    slack = jnp.minimum(lengths[source_of] - 1, reach - lengths[taker]) // 2
    slack = jnp.where((source_of == sequence[0]) | (taker == sequence[0]) | (lengths[taker] == 0), 0, jnp.maximum(slack, 0))
    passed = jax.random.randint(jax.random.fold_in(own, 4), (number_of // 2,), 0, 1 << 20) % (slack + 1)
    lengths = lengths.at[source_of].add(-passed).at[taker].add(passed)
    items = jnp.searchsorted(jnp.cumsum(lengths), jnp.arange(rows * top), side="right").astype(jnp.int32)
    listing = items.reshape(top, rows).T
    listing = listing[jax.random.permutation(jax.random.fold_in(own, 1), rows)]
    offset_by = jax.random.randint(jax.random.fold_in(own, 2), (rows, 1), 0, top)
    return jnp.take_along_axis(listing, (jnp.arange(top)[None, :] + offset_by) % top, axis=1)


def load_shares(number_of, total, limit, skew, full):
    portions = [(1 << 20) // math.isqrt(grade ** skew) + 1 for grade in range(1, number_of + 1)]
    largest = limit if full else min(limit, max(-(-total // number_of), total * portions[0] // sum(portions)))
    least = 1 if total - largest >= number_of - 1 else 0
    holding, rest = [largest] + [least] * (number_of - 1), total - largest - least * (number_of - 1)
    while rest > 0:
        free = [i for i in range(1, number_of) if holding[i] < largest] or [i for i in range(1, number_of) if holding[i] < limit]
        mass, remaining = sum([portions[i] for i in free]), rest
        for i in free:
            extra = min(limit - holding[i], max(1, remaining * portions[i] // mass), rest)
            holding[i] = holding[i] + extra
            rest = rest - extra
    return np.array(holding)


def bell_draw(own_key, dims, spread, reach, cuts=(), kind=jnp.bfloat16):
    entries = spread * jax.random.normal(own_key, dims, jnp.float32)
    if cuts:
        entries = entries * level_of(own_key, dims, cuts, -0.22, 0.18)
    return jnp.clip(entries, -reach, reach).astype(kind)


def setup_inputs(seed: int = 0, part: int = 0) -> dict:
    streams_of = jax.random.split(jax.random.key(seed), 7)
    own_keys = jax.random.split(jax.random.fold_in(streams_of[6], part), 7)
    activations = bell_draw(own_keys[0], (SPANS, SPAN, 2 * D), 1.0, 6.0, ((1, 16),))
    enc_weight = bell_draw(own_keys[1], (BLOCKS, 2 * D, BW), (2 * D) ** -0.5, 0.0625, ((0, 16),))
    enc_bias = bell_draw(own_keys[2], (BLOCKS, BW), 0.5, 3.0, ((0, 16),), jnp.float32)
    dec_weight = bell_draw(own_keys[3], (BLOCKS, BW, 2 * D), BW ** -0.5, 0.5, ((0, 16),))
    dec_bias = bell_draw(own_keys[4], (2 * D,), 0.5, 3.0, (), jnp.float32)
    active_keys = jax.random.split(jax.random.fold_in(own_keys[5], 1), SPANS // SPANS)
    active_turns = jax.random.permutation(jax.random.fold_in(own_keys[5], 3), SPANS // SPANS)
    active = jax.vmap(lambda own, number: deal_out(jax.random.fold_in(own_keys[5], 2), own, number, SPANS, BLOCKS, K, MOST, 2))(active_keys, active_turns).reshape((SPANS, K))
    return dict(activations=activations, enc_weight=enc_weight, enc_bias=enc_bias, dec_weight=dec_weight, dec_bias=dec_bias, active=active)


penalty_weight = 0.1
grad_scale = 0.0625
epsilon = 1e-06

def slot_tables(active):
    blocks = jnp.arange(BLOCKS, dtype=jnp.int32)
    member = jnp.any(active[:, :, None] == blocks[None, None, :], axis=1).astype(jnp.int32)
    position = jnp.cumsum(member, axis=0) - member
    slot_index = jnp.arange(MOST, dtype=jnp.int32)
    chosen = member[:, :, None] * (position[:, :, None] == slot_index[None, None, :]).astype(jnp.int32)
    span_index = jnp.arange(SPANS, dtype=jnp.int32)
    span_of = lax.optimization_barrier(jnp.sum(chosen * span_index[:, None, None], axis=0)).astype(jnp.int32)
    validity = lax.optimization_barrier(jnp.sum(chosen, axis=0)).astype(jnp.float32)
    return (span_of, validity)

def reference(activations, enc_weight, enc_bias, dec_weight, dec_bias, active):
    span_of, validity = slot_tables(active)
    feature_width = 2 * D
    row_count = MOST * SPAN

    def gather_rows(source, block):
        return jnp.take(source, span_of[block], axis=0).reshape(row_count, feature_width)

    def live_rows(block):
        return jnp.repeat(validity[block], SPAN)[:, None]

    def forward(recon, block):
        token_rows = gather_rows(activations, block)
        preact = jnp.dot(token_rows, enc_weight[block], preferred_element_type=jnp.float32) + enc_bias[block]
        features = jnp.maximum(preact, 0.0) * live_rows(block)
        contrib = jnp.dot(features.astype(jnp.bfloat16), dec_weight[block], preferred_element_type=jnp.float32).astype(jnp.bfloat16)
        placed = contrib.astype(jnp.float32).reshape(MOST, SPAN, feature_width)
        recon = recon.at[span_of[block]].add(placed)
        return (recon, preact)
    start = jnp.zeros((SPANS, SPAN, feature_width), jnp.float32)
    block_ids = jnp.arange(BLOCKS, dtype=jnp.int32)
    recon, preacts = lax.scan(forward, start, block_ids)
    residue = recon + dec_bias - activations.astype(jnp.float32)
    scaled = residue * grad_scale
    deltas = scaled.astype(jnp.bfloat16)
    dec_bias_grad = lax.optimization_barrier(jnp.sum(scaled, axis=(0, 1)))

    def backward(inputs):
        block, preact = inputs
        token_rows = gather_rows(activations, block)
        delta_rows = gather_rows(deltas, block)
        live_mask = live_rows(block)
        features = jnp.maximum(preact, 0.0) * live_mask
        weights = dec_weight[block].astype(jnp.float32)
        base_norm = jnp.sqrt(lax.optimization_barrier(jnp.sum(weights[:, :D] * weights[:, :D], axis=1)) + epsilon)
        chat_norm = jnp.sqrt(lax.optimization_barrier(jnp.sum(weights[:, D:] * weights[:, D:], axis=1)) + epsilon)
        directions = jnp.concatenate([weights[:, :D] / base_norm[:, None], weights[:, D:] / chat_norm[:, None]], axis=1)
        feature_sum = lax.optimization_barrier(jnp.sum(features, axis=0))
        dec_grad = jnp.dot(features.astype(jnp.bfloat16).T, delta_rows, preferred_element_type=jnp.float32) + penalty_weight * feature_sum[:, None] * directions
        feature_grad = jnp.dot(delta_rows, dec_weight[block].T, preferred_element_type=jnp.float32) + penalty_weight * (base_norm + chat_norm)
        preact_grad = jnp.where(preact > 0.0, feature_grad, 0.0) * live_mask
        enc_grad = jnp.dot(token_rows.T, preact_grad.astype(jnp.bfloat16), preferred_element_type=jnp.float32)
        bias_grad = lax.optimization_barrier(jnp.sum(preact_grad, axis=0))
        return (enc_grad, bias_grad, dec_grad)
    enc_grad, enc_bias_grad, dec_grad = lax.map(backward, (block_ids, preacts))
    return (enc_grad, enc_bias_grad, dec_grad, dec_bias_grad)
```

```python
import functools

import jax
import jax.numpy as jnp
from jax import lax
from jax.experimental import pallas as pl
from jax.experimental.pallas import tpu as pltpu
from jax.sharding import PartitionSpec as P

MOST = 2
AXIS = "latent"

penalty_weight = 0.1
grad_scale = 0.0625
epsilon = 1e-06

f32 = jnp.float32
bf16 = jnp.bfloat16


def swap(x, distance, count):
    return lax.ppermute(x, AXIS, [(i, i ^ distance) for i in range(count)])


def exchange(x, groups=None):
    return lax.all_to_all(
        x, AXIS, split_axis=0, concat_axis=0, tiled=True, axis_index_groups=groups
    )


def slot_tables(active, count):
    blocks = jnp.arange(count, dtype=jnp.int32)
    member = jnp.any(active[:, :, None] == blocks[None, None, :], axis=1).astype(jnp.int32)
    position = jnp.cumsum(member, axis=0) - member
    slots = jnp.arange(MOST, dtype=jnp.int32)
    chosen = member[:, :, None] * (position[:, :, None] == slots).astype(jnp.int32)
    spans = jnp.arange(active.shape[0], dtype=jnp.int32)
    span_of = jnp.sum(chosen * spans[:, None, None], axis=0)
    live = jnp.sum(chosen, axis=0)
    named = active[:, :, None] == blocks[None, None, :]
    slot_of = jnp.sum(jnp.where(named, position[:, None, :], 0), axis=2)
    return span_of, live, slot_of


def copy_block(index_ref, source_ref, out_ref):
    out_ref[...] = source_ref[...]


def pick_spans(rows, index):
    span_count, part_rows, width = rows.shape
    picked = index.shape[0]
    return pl.pallas_call(
        copy_block,
        grid_spec=pltpu.PrefetchScalarGridSpec(
            num_scalar_prefetch=1,
            grid=(picked,),
            in_specs=[pl.BlockSpec((1, part_rows, width), lambda i, at: (at[i], 0, 0))],
            out_specs=pl.BlockSpec((1, part_rows, width), lambda i, at: (i, 0, 0)),
        ),
        out_shape=jax.ShapeDtypeStruct((picked, part_rows, width), rows.dtype),
        name="pick_spans",
    )(index, rows)


def decode_kernel(names, skipped, place_ref, block_ref, core_ref, feat_ref, dec_ref, r_ref, y_ref, total):
    span_count = place_ref.shape[0] // names
    width = dec_ref.shape[-1]
    r_ref[...] = jnp.zeros_like(r_ref)
    total[...] = jnp.zeros_like(total)

    def span_step(span, carry):
        feats, decs, recon = [], [], None
        for name in range(names):
            feat = feat_ref[place_ref[span * names + name]]
            dec = dec_ref[block_ref[span * names + name]]
            contrib = jnp.dot(feat, dec, preferred_element_type=f32).astype(bf16).astype(f32)
            recon = contrib if recon is None else recon + contrib
            feats.append(feat)
            decs.append(dec)
        scaled = recon * grad_scale
        if skipped:
            lane = lax.broadcasted_iota(jnp.int32, scaled.shape, 1)
            scaled = jnp.where(lane >= core_ref[0] * skipped, scaled, 0.0)
        delta = scaled.astype(bf16)
        for name in range(names):
            part = lax.dot_general(
                delta, decs[name], (((1,), (1,)), ((), ())), preferred_element_type=f32
            )
            r_ref[place_ref[span * names + name]] = part.astype(bf16)
            grad = lax.dot_general(
                feats[name], delta, (((0,), (0,)), ((), ())), preferred_element_type=f32
            )
            total[block_ref[span * names + name]] += grad
        return carry

    lax.fori_loop(0, span_count, span_step, 0)
    y_ref[...] = total[...].astype(bf16)


def decode(names, skipped, place, block, core, feats, dec):
    vmem = pl.BlockSpec(memory_space=pltpu.VMEM)
    smem = pl.BlockSpec(memory_space=pltpu.SMEM)
    pairs, rows, latents, columns = place.shape[0], feats.shape[1], feats.shape[2], dec.shape[2]
    return pl.pallas_call(
        functools.partial(decode_kernel, names, skipped),
        in_specs=[smem, smem, smem, vmem, vmem],
        out_specs=[vmem, vmem],
        out_shape=[
            jax.ShapeDtypeStruct(feats.shape, bf16),
            jax.ShapeDtypeStruct(dec.shape, bf16),
        ],
        scratch_shapes=[pltpu.VMEM(dec.shape, f32)],
        compiler_params=pltpu.CompilerParams(vmem_limit_bytes=56 * 2**20),
        cost_estimate=pl.CostEstimate(
            flops=6 * pairs * rows * latents * columns,
            bytes_accessed=4 * (feats.size + dec.size),
            transcendentals=0,
        ),
        name="decode",
    )(place, block, core, feats, dec)


def decode_plain(names, skipped, place, block, core, feats, dec):
    span_count = place.shape[0] // names
    r_out = jnp.zeros(feats.shape, bf16)
    total = jnp.zeros(dec.shape, f32)
    width = dec.shape[-1]
    keep = (jnp.arange(width) >= core[0] * skipped).astype(f32)

    def span_step(span, carry):
        r_out, total = carry
        at = lax.dynamic_slice(place, (span * names,), (names,))
        which = lax.dynamic_slice(block, (span * names,), (names,))
        feat, mine = feats[at], dec[which]
        contrib = jnp.einsum("krl,klc->krc", feat, mine, preferred_element_type=f32).astype(bf16)
        recon = jnp.sum(contrib.astype(f32), axis=0)
        delta = (recon * grad_scale * keep).astype(bf16)
        part = jnp.einsum("rc,klc->krl", delta, mine, preferred_element_type=f32)
        grad = jnp.einsum("krl,rc->klc", feat, delta, preferred_element_type=f32)
        return r_out.at[at].set(part.astype(bf16)), total.at[which].add(grad)

    r_out, total = lax.fori_loop(0, span_count, span_step, (r_out, total))
    return r_out, total.astype(bf16)


def shards(activations, enc_weight, enc_bias, dec_weight, dec_bias, active):
    count = lax.axis_size(AXIS)
    me = lax.axis_index(AXIS)
    span_count, part_rows, width = activations.shape
    names = active.shape[1]
    latents = enc_weight.shape[-1]
    stream = width // 2
    half, chips = count // 2, count // 2
    halves = [[h * half + i for i in range(half)] for h in range(2)]
    same_core = [[2 * i + c for i in range(chips)] for c in range(2)]
    my_half, core = me // half, me % 2
    enc, dec = enc_weight[0], dec_weight[0]
    span_of, live, slot_of = slot_tables(active, count)

    mine = lax.dynamic_slice(span_of, (my_half * half, 0), (half, MOST)).reshape(-1)
    far = [swap(activations[:, :, i * stream : (i + 1) * stream], half, count) for i in range(2)]
    shape = (half, MOST, part_rows)
    x_own = exchange(pick_spans(activations, mine).reshape(shape + (width,)), halves)
    x_far = [exchange(pick_spans(a, mine).reshape(shape + (stream,)), halves) for a in far]

    per_chip = width // chips
    if per_chip % 128 == 0:
        window = -(-(per_chip // 2) // 128) * 128
    else:
        window = per_chip // 2
    skipped = 2 * window - per_chip
    starts = [(i // 2) * per_chip + (i % 2) * (per_chip - window) for i in range(count)]
    dec_all = exchange(jnp.stack([dec[:, s : s + window] for s in starts]))

    rows = half * MOST * part_rows
    own = x_own.reshape(rows, width)
    far = [x.reshape(rows, stream) for x in x_far]
    dot = functools.partial(jnp.dot, preferred_element_type=f32)
    preact_own = dot(own, enc) + enc_bias[0]
    preact_far = dot(far[0], enc[:stream]) + dot(far[1], enc[stream:]) + enc_bias[0]
    my_live = lax.dynamic_slice(live, (me, 0), (1, MOST)).astype(f32)
    mask = jnp.broadcast_to(my_live[0][None, :, None, None], shape + (1,)).reshape(rows, 1)
    feat_own = jnp.maximum(preact_own, 0.0) * mask
    feat_far = jnp.maximum(preact_far, 0.0) * mask
    fb_own, fb_far = feat_own.astype(bf16), feat_far.astype(bf16)

    def by_slot(x):
        return x.reshape(half, MOST, part_rows, latents).transpose(1, 0, 2, 3).reshape(MOST, -1, latents)

    def by_source(x):
        return x.reshape(MOST, half, part_rows, latents).transpose(1, 0, 2, 3).reshape(rows, latents)

    lower = my_half == 0
    a, b = by_slot(fb_own), by_slot(fb_far)
    feats = jnp.concatenate([jnp.where(lower, a, b), jnp.where(lower, b, a)], axis=1)

    span_rows = feats.shape[1]
    same = exchange(jnp.broadcast_to(feats[None], (chips,) + feats.shape), same_core)
    other = swap(same, 1, count)
    feats_all = jnp.concatenate([same, other]).reshape(count * MOST, span_rows, latents)
    place = (((active % 2) ^ core) * chips + active // 2) * MOST + slot_of

    small = feats_all.size * 4 + dec_all.size * 8 < 40 * 2**20
    r_out, y_out = (decode if small else decode_plain)(
        names, skipped, place.reshape(-1), active.reshape(-1), core.reshape(1), feats_all, dec_all
    )
    r_out = r_out.reshape(2, chips, MOST, span_rows, latents)
    r_near = swap(r_out[1], 1, count)
    r_sum = (r_out[0].astype(f32) + r_near.astype(f32)).astype(bf16)
    r_in = exchange(r_sum, same_core)
    y_in = exchange(y_out)
    recon_part = jnp.sum(r_in.astype(f32), axis=0)

    weights = dec.astype(f32)
    base_norm = jnp.sqrt(jnp.sum(weights[:, :stream] * weights[:, :stream], axis=1) + epsilon)
    chat_norm = jnp.sqrt(jnp.sum(weights[:, stream:] * weights[:, stream:], axis=1) + epsilon)
    bias_dec = jnp.sum(weights * dec_bias[None, :], axis=1)
    constant = grad_scale * bias_dec + penalty_weight * (base_norm + chat_norm)
    cross = functools.partial(
        lax.dot_general, dimension_numbers=(((1,), (1,)), ((), ())), preferred_element_type=f32
    )
    xd_own = cross(own, dec)
    xd_far = cross(far[0], dec[:, :stream]) + cross(far[1], dec[:, stream:])
    down = functools.partial(
        lax.dot_general, dimension_numbers=(((0,), (0,)), ((), ())), preferred_element_type=f32
    )
    fx = down(fb_own, own) + jnp.concatenate([down(fb_far, x) for x in far], axis=1)
    feature_sum = jnp.sum(feat_own, axis=0) + jnp.sum(feat_far, axis=0)
    rounded_sum = jnp.sum(fb_own.astype(f32), axis=0) + jnp.sum(fb_far.astype(f32), axis=0)
    inverse = jnp.concatenate(
        [
            jnp.broadcast_to(1.0 / base_norm[:, None], (latents, stream)),
            jnp.broadcast_to(1.0 / chat_norm[:, None], (latents, stream)),
        ],
        axis=1,
    )
    dec_part = (
        grad_scale * (rounded_sum[:, None] * dec_bias[None, :] - fx)
        + penalty_weight * feature_sum[:, None] * weights * inverse
    )

    act_sum = jnp.sum(activations.astype(f32), axis=(0, 1))
    bias_part = jnp.sum(rounded_sum[:, None] * weights, axis=0) - act_sum
    bias_cols = jnp.sum(exchange(bias_part.reshape(count, width // count)), axis=0)
    bias_all = exchange(jnp.broadcast_to(bias_cols[None], (count, width // count))).reshape(-1)
    dec_bias_grad = grad_scale * (bias_all + float(span_count * part_rows * count) * dec_bias)

    first, second = recon_part[:, : span_rows // 2], recon_part[:, span_rows // 2 :]
    r_own = by_source(jnp.where(lower, first, second))
    r_far = by_source(jnp.where(lower, second, first))
    grad_own = jnp.where((preact_own > 0.0) & (mask > 0.0), r_own - grad_scale * xd_own + constant, 0.0)
    grad_far = jnp.where((preact_far > 0.0) & (mask > 0.0), r_far - grad_scale * xd_far + constant, 0.0)
    bias_grad = jnp.sum(grad_own, axis=0) + jnp.sum(grad_far, axis=0)
    gb_own, gb_far = grad_own.astype(bf16), grad_far.astype(bf16)
    enc_grad = down(own, gb_own) + jnp.concatenate([down(x, gb_far) for x in far], axis=0)

    y_cols = jnp.concatenate(
        [y_in[i] if i % 2 == 0 else y_in[i][:, skipped:] for i in range(count)], axis=1
    )
    dec_grad = dec_part + y_cols.astype(f32)
    return (enc_grad[None], bias_grad[None], dec_grad[None], dec_bias_grad)


def solution(mesh):
    in_specs = (
        P("group", "latent", None),
        P(("group", "latent"), None, None),
        P(("group", "latent"), None),
        P(("group", "latent"), None, None),
        P("group"),
        P("group", None),
    )
    out_specs = (
        P(("group", "latent"), None, None),
        P(("group", "latent"), None),
        P(("group", "latent"), None, None),
        P("group"),
    )
    return jax.shard_map(shards, mesh=mesh, in_specs=in_specs, out_specs=out_specs, check_vma=False)
```

```python
import functools

import jax
import jax.numpy as jnp
from jax import lax
from jax.experimental import pallas as pl
from jax.experimental.pallas import tpu as pltpu
from jax.sharding import PartitionSpec as P

MOST = 2
AXIS = "latent"

penalty_weight = 0.1
grad_scale = 0.0625
epsilon = 1e-06

f32 = jnp.float32
bf16 = jnp.bfloat16


def swap(x, distance, count):
    return lax.ppermute(x, AXIS, [(i, i ^ distance) for i in range(count)])


def exchange(x, groups=None):
    return lax.all_to_all(
        x, AXIS, split_axis=0, concat_axis=0, tiled=True, axis_index_groups=groups
    )


def slot_tables(active, count):
    blocks = jnp.arange(count, dtype=jnp.int32)
    member = jnp.any(active[:, :, None] == blocks[None, None, :], axis=1).astype(jnp.int32)
    position = jnp.cumsum(member, axis=0) - member
    slots = jnp.arange(MOST, dtype=jnp.int32)
    chosen = member[:, :, None] * (position[:, :, None] == slots).astype(jnp.int32)
    spans = jnp.arange(active.shape[0], dtype=jnp.int32)
    span_of = jnp.sum(chosen * spans[:, None, None], axis=0)
    live = jnp.sum(chosen, axis=0)
    named = active[:, :, None] == blocks[None, None, :]
    slot_of = jnp.sum(jnp.where(named, position[:, None, :], 0), axis=2)
    return span_of, live, slot_of


def pick_kernel(index_ref, rows_ref, out_ref, sems):
    picked = out_ref.shape[0]

    def start(i, carry):
        pltpu.make_async_copy(rows_ref.at[index_ref[i]], out_ref.at[i], sems.at[i]).start()
        return carry

    def wait(i, carry):
        pltpu.make_async_copy(rows_ref.at[0], out_ref.at[i], sems.at[i]).wait()
        return carry

    lax.fori_loop(0, picked, start, 0)
    lax.fori_loop(0, picked, wait, 0)


def pick_spans(rows, index):
    shape = (index.shape[0],) + rows.shape[1:]
    return pl.pallas_call(
        pick_kernel,
        in_specs=[pl.BlockSpec(memory_space=pltpu.SMEM), pl.BlockSpec(memory_space=pl.ANY)],
        out_specs=pl.BlockSpec(memory_space=pl.ANY),
        out_shape=jax.ShapeDtypeStruct(shape, rows.dtype),
        scratch_shapes=[pltpu.SemaphoreType.DMA((shape[0],))],
        name="pick_spans",
    )(index, rows)


def window_kernel(starts, dec_ref, out_ref, sems):
    width = out_ref.shape[-1]
    copies = [
        pltpu.make_async_copy(dec_ref.at[:, pl.ds(s, width)], out_ref.at[i], sems.at[i])
        for i, s in enumerate(starts)
    ]
    for copy in copies:
        copy.start()
    for copy in copies:
        copy.wait()


def cut_windows(dec, starts, window):
    if any(s % 128 for s in starts) or window % 128:
        return jnp.stack([dec[:, s : s + window] for s in starts])
    return pl.pallas_call(
        functools.partial(window_kernel, starts),
        in_specs=[pl.BlockSpec(memory_space=pl.ANY)],
        out_specs=pl.BlockSpec(memory_space=pl.ANY),
        out_shape=jax.ShapeDtypeStruct((len(starts), dec.shape[0], window), dec.dtype),
        scratch_shapes=[pltpu.SemaphoreType.DMA((len(starts),))],
        name="cut_windows",
    )(dec)


def join_kernel(skipped, part_ref, y_ref, out_ref):
    window = y_ref.shape[-1]
    out_ref[:, :window] = part_ref[:, :window] + y_ref[0].astype(f32)
    out_ref[:, window:] = part_ref[:, window:] + y_ref[1][:, skipped:].astype(f32)


def join_windows(part, y, skipped):
    count, latents, window = y.shape
    if window % 128 or skipped % 128:
        cols = [y[i] if i % 2 == 0 else y[i][:, skipped:] for i in range(count)]
        return part + jnp.concatenate(cols, axis=1).astype(f32)
    per_chip = 2 * window - skipped
    return pl.pallas_call(
        functools.partial(join_kernel, skipped),
        grid=(count // 2,),
        in_specs=[
            pl.BlockSpec((latents, per_chip), lambda i: (0, i)),
            pl.BlockSpec((2, latents, window), lambda i: (i, 0, 0)),
        ],
        out_specs=pl.BlockSpec((latents, per_chip), lambda i: (0, i)),
        out_shape=jax.ShapeDtypeStruct(part.shape, f32),
        name="join_windows",
    )(part, y)


def decode_kernel(names, skipped, place_ref, block_ref, core_ref, feat_ref, dec_ref, r_ref, y_ref, total, feats, decs):
    span_count = place_ref.shape[0] // names
    latents = feat_ref.shape[-1]
    r_ref[...] = jnp.zeros_like(r_ref)
    total[...] = jnp.zeros_like(total)

    def span_step(span, carry):
        at = [place_ref[span * names + name] for name in range(names)]
        block = [block_ref[span * names + name] for name in range(names)]
        for name in range(names):
            feats[:, name * latents : (name + 1) * latents] = feat_ref[at[name]]
            decs[name * latents : (name + 1) * latents, :] = dec_ref[block[name]]
        scaled = jnp.dot(feats[...], decs[...], preferred_element_type=f32) * grad_scale
        if skipped:
            lane = lax.broadcasted_iota(jnp.int32, scaled.shape, 1)
            scaled = jnp.where(lane >= core_ref[0] * skipped, scaled, 0.0)
        delta = scaled.astype(bf16)
        part = lax.dot_general(
            delta, decs[...], (((1,), (1,)), ((), ())), preferred_element_type=f32
        ).astype(bf16)
        grad = lax.dot_general(
            feats[...], delta, (((0,), (0,)), ((), ())), preferred_element_type=f32
        )
        for name in range(names):
            r_ref[at[name]] = part[:, name * latents : (name + 1) * latents]
            total[block[name]] += grad[name * latents : (name + 1) * latents]
        return carry

    lax.fori_loop(0, span_count, span_step, 0)
    y_ref[...] = total[...].astype(bf16)


def decode(names, skipped, place, block, core, feats, dec):
    vmem = pl.BlockSpec(memory_space=pltpu.VMEM)
    smem = pl.BlockSpec(memory_space=pltpu.SMEM)
    pairs, rows, latents, columns = place.shape[0], feats.shape[1], feats.shape[2], dec.shape[2]
    return pl.pallas_call(
        functools.partial(decode_kernel, names, skipped),
        in_specs=[smem, smem, smem, vmem, vmem],
        out_specs=[vmem, vmem],
        out_shape=[
            jax.ShapeDtypeStruct(feats.shape, bf16),
            jax.ShapeDtypeStruct(dec.shape, bf16),
        ],
        scratch_shapes=[
            pltpu.VMEM(dec.shape, f32),
            pltpu.VMEM((rows, names * latents), bf16),
            pltpu.VMEM((names * latents, columns), bf16),
        ],
        compiler_params=pltpu.CompilerParams(vmem_limit_bytes=56 * 2**20),
        cost_estimate=pl.CostEstimate(
            flops=6 * pairs * rows * latents * columns,
            bytes_accessed=4 * (feats.size + dec.size),
            transcendentals=0,
        ),
        name="decode",
    )(place, block, core, feats, dec)


def decode_plain(names, skipped, place, block, core, feats, dec):
    span_count = place.shape[0] // names
    r_out = jnp.zeros(feats.shape, bf16)
    total = jnp.zeros(dec.shape, f32)
    width = dec.shape[-1]
    keep = (jnp.arange(width) >= core[0] * skipped).astype(f32)

    def span_step(span, carry):
        r_out, total = carry
        at = lax.dynamic_slice(place, (span * names,), (names,))
        which = lax.dynamic_slice(block, (span * names,), (names,))
        feat, mine = feats[at], dec[which]
        contrib = jnp.einsum("krl,klc->krc", feat, mine, preferred_element_type=f32).astype(bf16)
        recon = jnp.sum(contrib.astype(f32), axis=0)
        delta = (recon * grad_scale * keep).astype(bf16)
        part = jnp.einsum("rc,klc->krl", delta, mine, preferred_element_type=f32)
        grad = jnp.einsum("krl,rc->klc", feat, delta, preferred_element_type=f32)
        return r_out.at[at].set(part.astype(bf16)), total.at[which].add(grad)

    r_out, total = lax.fori_loop(0, span_count, span_step, (r_out, total))
    return r_out, total.astype(bf16)


def shards(activations, enc_weight, enc_bias, dec_weight, dec_bias, active):
    count = lax.axis_size(AXIS)
    me = lax.axis_index(AXIS)
    span_count, part_rows, width = activations.shape
    names = active.shape[1]
    latents = enc_weight.shape[-1]
    stream = width // 2
    half, chips = count // 2, count // 2
    halves = [[h * half + i for i in range(half)] for h in range(2)]
    same_core = [[2 * i + c for i in range(chips)] for c in range(2)]
    my_half, core = me // half, me % 2
    enc, dec = enc_weight[0], dec_weight[0]
    span_of, live, slot_of = slot_tables(active, count)

    per_chip = width // chips
    if per_chip % 128 == 0:
        window = -(-(per_chip // 2) // 128) * 128
    else:
        window = per_chip // 2
    skipped = 2 * window - per_chip
    starts = [(i // 2) * per_chip + (i % 2) * (per_chip - window) for i in range(count)]
    dec_all = exchange(cut_windows(dec, starts, window))

    mine = lax.dynamic_slice(span_of, (my_half * half, 0), (half, MOST)).reshape(-1)
    across = swap(activations, half, count)
    shape = (half, MOST, part_rows)
    near, dec_all = lax.optimization_barrier((pick_spans(activations, mine), dec_all))
    x_own = exchange(near.reshape(shape + (width,)), halves)
    across, x_own = lax.optimization_barrier((pick_spans(across, mine), x_own))
    x_far = exchange(across.reshape(shape + (width,)), halves)

    rows = half * MOST * part_rows
    own = x_own.reshape(rows, width)
    far = x_far.reshape(rows, width)
    dot = functools.partial(jnp.dot, preferred_element_type=f32)
    preact_own = dot(own, enc) + enc_bias[0]
    preact_far = dot(far, enc) + enc_bias[0]
    my_live = lax.dynamic_slice(live, (me, 0), (1, MOST)).astype(f32)
    mask = jnp.broadcast_to(my_live[0][None, :, None, None], shape + (1,)).reshape(rows, 1)
    feat_own = jnp.maximum(preact_own, 0.0) * mask
    feat_far = jnp.maximum(preact_far, 0.0) * mask
    fb_own, fb_far = feat_own.astype(bf16), feat_far.astype(bf16)

    def by_slot(x):
        return x.reshape(half, MOST, part_rows, latents).transpose(1, 0, 2, 3).reshape(MOST, -1, latents)

    def by_source(x):
        return x.reshape(MOST, half, part_rows, latents).transpose(1, 0, 2, 3).reshape(rows, latents)

    lower = my_half == 0
    a, b = by_slot(fb_own), by_slot(fb_far)
    feats = jnp.concatenate([jnp.where(lower, a, b), jnp.where(lower, b, a)], axis=1)

    span_rows = feats.shape[1]
    same = exchange(jnp.broadcast_to(feats[None], (chips,) + feats.shape), same_core)
    other = swap(same, 1, count)
    feats_all = jnp.concatenate([same, other]).reshape(count * MOST, span_rows, latents)
    place = (((active % 2) ^ core) * chips + active // 2) * MOST + slot_of

    small = feats_all.size * 4 + dec_all.size * 8 < 40 * 2**20
    r_out, y_out = (decode if small else decode_plain)(
        names, skipped, place.reshape(-1), active.reshape(-1), core.reshape(1), feats_all, dec_all
    )
    r_out = r_out.reshape(2, chips, MOST, span_rows, latents)
    r_near = swap(r_out[1], 1, count)
    r_sum = (r_out[0].astype(f32) + r_near.astype(f32)).astype(bf16)
    r_in, y_out = lax.optimization_barrier((exchange(r_sum, same_core), y_out))
    y_in = exchange(y_out)
    recon_part = jnp.sum(r_in.astype(f32), axis=0)

    weights = dec.astype(f32)
    base_norm = jnp.sqrt(jnp.sum(weights[:, :stream] * weights[:, :stream], axis=1) + epsilon)
    chat_norm = jnp.sqrt(jnp.sum(weights[:, stream:] * weights[:, stream:], axis=1) + epsilon)
    bias_dec = jnp.sum(weights * dec_bias[None, :], axis=1)
    constant = grad_scale * bias_dec + penalty_weight * (base_norm + chat_norm)
    cross = functools.partial(
        lax.dot_general, dimension_numbers=(((1,), (1,)), ((), ())), preferred_element_type=f32
    )
    xd_own = cross(own, dec)
    xd_far = cross(far, dec)
    down = functools.partial(
        lax.dot_general, dimension_numbers=(((0,), (0,)), ((), ())), preferred_element_type=f32
    )
    fx = down(fb_own, own) + down(fb_far, far)
    feature_sum = jnp.sum(feat_own, axis=0) + jnp.sum(feat_far, axis=0)
    rounded_sum = jnp.sum(fb_own.astype(f32), axis=0) + jnp.sum(fb_far.astype(f32), axis=0)
    inverse = jnp.concatenate(
        [
            jnp.broadcast_to(1.0 / base_norm[:, None], (latents, stream)),
            jnp.broadcast_to(1.0 / chat_norm[:, None], (latents, stream)),
        ],
        axis=1,
    )
    dec_part = (
        grad_scale * (rounded_sum[:, None] * dec_bias[None, :] - fx)
        + penalty_weight * feature_sum[:, None] * weights * inverse
    )

    first, second = recon_part[:, : span_rows // 2], recon_part[:, span_rows // 2 :]
    r_own = by_source(jnp.where(lower, first, second))
    r_far = by_source(jnp.where(lower, second, first))
    grad_own = jnp.where((preact_own > 0.0) & (mask > 0.0), r_own - grad_scale * xd_own + constant, 0.0)
    grad_far = jnp.where((preact_far > 0.0) & (mask > 0.0), r_far - grad_scale * xd_far + constant, 0.0)
    bias_grad = jnp.sum(grad_own, axis=0) + jnp.sum(grad_far, axis=0)
    gb_own, gb_far = grad_own.astype(bf16), grad_far.astype(bf16)
    enc_grad = down(own, gb_own) + down(far, gb_far)

    act_sum = jnp.sum(activations.astype(f32), axis=(0, 1))
    bias_sum = jnp.sum(rounded_sum[:, None] * weights, axis=0) - act_sum
    bias_sum, recon_part = lax.optimization_barrier((bias_sum, recon_part))
    distance = 1
    while distance < count:
        bias_sum = bias_sum + swap(bias_sum, distance, count)
        distance *= 2
    dec_bias_grad = grad_scale * (bias_sum + float(span_count * part_rows * count) * dec_bias)
    dec_grad = join_windows(dec_part, y_in, skipped)
    return (enc_grad[None], bias_grad[None], dec_grad[None], dec_bias_grad)


def solution(mesh):
    in_specs = (
        P("group", "latent", None),
        P(("group", "latent"), None, None),
        P(("group", "latent"), None),
        P(("group", "latent"), None, None),
        P("group"),
        P("group", None),
    )
    out_specs = (
        P(("group", "latent"), None, None),
        P(("group", "latent"), None),
        P(("group", "latent"), None, None),
        P("group"),
    )
    return jax.shard_map(shards, mesh=mesh, in_specs=in_specs, out_specs=out_specs, check_vma=False)
```

```python
import functools

import jax
import jax.numpy as jnp
from jax import lax
from jax.experimental import pallas as pl
from jax.experimental.pallas import tpu as pltpu
from jax.sharding import PartitionSpec as P

MOST = 2
AXIS = "latent"

penalty_weight = 0.1
grad_scale = 0.0625
epsilon = 1e-06

f32 = jnp.float32
bf16 = jnp.bfloat16


def swap(x, distance, count):
    return lax.ppermute(x, AXIS, [(i, i ^ distance) for i in range(count)])


def exchange(x, groups=None):
    return lax.all_to_all(
        x, AXIS, split_axis=0, concat_axis=0, tiled=True, axis_index_groups=groups
    )


def slot_tables(active, count):
    blocks = jnp.arange(count, dtype=jnp.int32)
    member = jnp.any(active[:, :, None] == blocks[None, None, :], axis=1).astype(jnp.int32)
    position = jnp.cumsum(member, axis=0) - member
    slots = jnp.arange(MOST, dtype=jnp.int32)
    chosen = member[:, :, None] * (position[:, :, None] == slots).astype(jnp.int32)
    spans = jnp.arange(active.shape[0], dtype=jnp.int32)
    span_of = jnp.sum(chosen * spans[:, None, None], axis=0)
    live = jnp.sum(chosen, axis=0)
    named = active[:, :, None] == blocks[None, None, :]
    slot_of = jnp.sum(jnp.where(named, position[:, None, :], 0), axis=2)
    return span_of, live, slot_of


def pick_kernel(firsts, index_ref, *refs):
    parts, out_ref, sems = refs[: len(firsts)], refs[-2], refs[-1]
    picked = out_ref.shape[0]

    def start(i, carry):
        span = index_ref[i]
        for first, part in zip(firsts, parts):

            @pl.when((span >= first) & (span < first + part.shape[0]))
            def _():
                pltpu.make_async_copy(part.at[span - first], out_ref.at[i], sems.at[i]).start()

        return carry

    def wait(i, carry):
        pltpu.make_async_copy(parts[0].at[0], out_ref.at[i], sems.at[i]).wait()
        return carry

    lax.fori_loop(0, picked, start, 0)
    lax.fori_loop(0, picked, wait, 0)


def pick_spans(parts, index):
    shape = (index.shape[0],) + parts[0].shape[1:]
    firsts = [sum(p.shape[0] for p in parts[:i]) for i in range(len(parts))]
    size = sum(p.size for p in parts) * 2
    return pl.pallas_call(
        functools.partial(pick_kernel, firsts),
        in_specs=[pl.BlockSpec(memory_space=pltpu.SMEM)]
        + [pl.BlockSpec(memory_space=pltpu.VMEM)] * len(parts),
        out_specs=pl.BlockSpec(memory_space=pl.ANY),
        out_shape=jax.ShapeDtypeStruct(shape, parts[0].dtype),
        scratch_shapes=[pltpu.SemaphoreType.DMA((shape[0],))],
        compiler_params=pltpu.CompilerParams(vmem_limit_bytes=48 * 2**20),
        cost_estimate=pl.CostEstimate(flops=0, bytes_accessed=3 * size, transcendentals=0),
        name="pick_spans",
    )(index, *parts)


def window_kernel(starts, dec_ref, out_ref, sems):
    width = out_ref.shape[-1]
    copies = [
        pltpu.make_async_copy(dec_ref.at[:, pl.ds(s, width)], out_ref.at[i], sems.at[i])
        for i, s in enumerate(starts)
    ]
    for copy in copies:
        copy.start()
    for copy in copies:
        copy.wait()


def cut_windows(dec, starts, window):
    if any(s % 128 for s in starts) or window % 128:
        return jnp.stack([dec[:, s : s + window] for s in starts])
    return pl.pallas_call(
        functools.partial(window_kernel, starts),
        in_specs=[pl.BlockSpec(memory_space=pltpu.VMEM)],
        out_specs=pl.BlockSpec(memory_space=pl.ANY),
        out_shape=jax.ShapeDtypeStruct((len(starts), dec.shape[0], window), dec.dtype),
        scratch_shapes=[pltpu.SemaphoreType.DMA((len(starts),))],
        cost_estimate=pl.CostEstimate(flops=0, bytes_accessed=4 * dec.size, transcendentals=0),
        name="cut_windows",
    )(dec)


def join_kernel(skipped, part_ref, y_ref, out_ref):
    window = y_ref.shape[-1]
    out_ref[:, :window] = part_ref[:, :window] + y_ref[0].astype(f32)
    out_ref[:, window:] = part_ref[:, window:] + y_ref[1][:, skipped:].astype(f32)


def join_windows(part, y, skipped):
    count, latents, window = y.shape
    if window % 128 or skipped % 128:
        cols = [y[i] if i % 2 == 0 else y[i][:, skipped:] for i in range(count)]
        return part + jnp.concatenate(cols, axis=1).astype(f32)
    per_chip = 2 * window - skipped
    return pl.pallas_call(
        functools.partial(join_kernel, skipped),
        grid=(count // 2,),
        in_specs=[
            pl.BlockSpec((latents, per_chip), lambda i: (0, i)),
            pl.BlockSpec((2, latents, window), lambda i: (i, 0, 0)),
        ],
        out_specs=pl.BlockSpec((latents, per_chip), lambda i: (0, i)),
        out_shape=jax.ShapeDtypeStruct(part.shape, f32),
        name="join_windows",
    )(part, y)


def decode_kernel(names, skipped, place_ref, block_ref, core_ref, feat_ref, dec_ref, r_ref, y_ref, total, feats, decs):
    span_count = place_ref.shape[0] // names
    latents = feat_ref.shape[-1]
    r_ref[...] = jnp.zeros_like(r_ref)
    total[...] = jnp.zeros_like(total)

    def span_step(span, carry):
        at = [place_ref[span * names + name] for name in range(names)]
        block = [block_ref[span * names + name] for name in range(names)]
        for name in range(names):
            feats[:, name * latents : (name + 1) * latents] = feat_ref[at[name]]
            decs[name * latents : (name + 1) * latents, :] = dec_ref[block[name]]
        scaled = jnp.dot(feats[...], decs[...], preferred_element_type=f32) * grad_scale
        if skipped:
            lane = lax.broadcasted_iota(jnp.int32, scaled.shape, 1)
            scaled = jnp.where(lane >= core_ref[0] * skipped, scaled, 0.0)
        delta = scaled.astype(bf16)
        part = lax.dot_general(
            delta, decs[...], (((1,), (1,)), ((), ())), preferred_element_type=f32
        ).astype(bf16)
        grad = lax.dot_general(
            feats[...], delta, (((0,), (0,)), ((), ())), preferred_element_type=f32
        )
        for name in range(names):
            r_ref[at[name]] = part[:, name * latents : (name + 1) * latents]
            total[block[name]] += grad[name * latents : (name + 1) * latents]
        return carry

    lax.fori_loop(0, span_count, span_step, 0)
    y_ref[...] = total[...].astype(bf16)


def decode(names, skipped, place, block, core, feats, dec):
    vmem = pl.BlockSpec(memory_space=pltpu.VMEM)
    smem = pl.BlockSpec(memory_space=pltpu.SMEM)
    pairs, rows, latents, columns = place.shape[0], feats.shape[1], feats.shape[2], dec.shape[2]
    return pl.pallas_call(
        functools.partial(decode_kernel, names, skipped),
        in_specs=[smem, smem, smem, vmem, vmem],
        out_specs=[vmem, vmem],
        out_shape=[
            jax.ShapeDtypeStruct(feats.shape, bf16),
            jax.ShapeDtypeStruct(dec.shape, bf16),
        ],
        scratch_shapes=[
            pltpu.VMEM(dec.shape, f32),
            pltpu.VMEM((rows, names * latents), bf16),
            pltpu.VMEM((names * latents, columns), bf16),
        ],
        compiler_params=pltpu.CompilerParams(vmem_limit_bytes=56 * 2**20),
        cost_estimate=pl.CostEstimate(
            flops=6 * pairs * rows * latents * columns,
            bytes_accessed=4 * (feats.size + dec.size),
            transcendentals=0,
        ),
        name="decode",
    )(place, block, core, feats, dec)


def decode_plain(names, skipped, place, block, core, feats, dec):
    span_count = place.shape[0] // names
    r_out = jnp.zeros(feats.shape, bf16)
    total = jnp.zeros(dec.shape, f32)
    width = dec.shape[-1]
    keep = (jnp.arange(width) >= core[0] * skipped).astype(f32)

    def span_step(span, carry):
        r_out, total = carry
        at = lax.dynamic_slice(place, (span * names,), (names,))
        which = lax.dynamic_slice(block, (span * names,), (names,))
        feat, mine = feats[at], dec[which]
        contrib = jnp.einsum("krl,klc->krc", feat, mine, preferred_element_type=f32).astype(bf16)
        recon = jnp.sum(contrib.astype(f32), axis=0)
        delta = (recon * grad_scale * keep).astype(bf16)
        part = jnp.einsum("rc,klc->krl", delta, mine, preferred_element_type=f32)
        grad = jnp.einsum("krl,rc->klc", feat, delta, preferred_element_type=f32)
        return r_out.at[at].set(part.astype(bf16)), total.at[which].add(grad)

    r_out, total = lax.fori_loop(0, span_count, span_step, (r_out, total))
    return r_out, total.astype(bf16)


def shards(activations, enc_weight, enc_bias, dec_weight, dec_bias, active):
    count = lax.axis_size(AXIS)
    me = lax.axis_index(AXIS)
    span_count, part_rows, width = activations.shape
    names = active.shape[1]
    latents = enc_weight.shape[-1]
    stream = width // 2
    half, chips = count // 2, count // 2
    halves = [[h * half + i for i in range(half)] for h in range(2)]
    same_core = [[2 * i + c for i in range(chips)] for c in range(2)]
    my_half, core = me // half, me % 2
    enc, dec = enc_weight[0], dec_weight[0]
    span_of, live, slot_of = slot_tables(active, count)

    per_chip = width // chips
    if per_chip % 128 == 0:
        window = -(-(per_chip // 2) // 128) * 128
    else:
        window = per_chip // 2
    skipped = 2 * window - per_chip
    starts = [(i // 2) * per_chip + (i % 2) * (per_chip - window) for i in range(count)]

    mine = lax.dynamic_slice(span_of, (my_half * half, 0), (half, MOST)).reshape(-1)
    first = (span_count * 5 + 7) // 8
    across = [swap(activations[:first], half, count), swap(activations[first:], half, count)]
    shape = (half, MOST, part_rows)
    x_own = exchange(pick_spans([activations], mine).reshape(shape + (width,)), halves)
    windows, across[0], x_own = lax.optimization_barrier(
        (cut_windows(dec, starts, window), across[0], x_own)
    )
    dec_all = exchange(windows)
    across[1], dec_all = lax.optimization_barrier((across[1], dec_all))
    x_far = exchange(pick_spans(across, mine).reshape(shape + (width,)), halves)

    rows = half * MOST * part_rows
    dot = functools.partial(jnp.dot, preferred_element_type=f32)
    my_live = lax.dynamic_slice(live, (me, 0), (1, MOST)).astype(f32)
    mask = jnp.broadcast_to(my_live[0][None, :, None, None], shape + (1,)).reshape(rows, 1)

    def by_slot(x):
        return x.reshape(half, MOST, part_rows, latents).transpose(1, 0, 2, 3).reshape(MOST, -1, latents)

    def by_source(x):
        return x.reshape(MOST, half, part_rows, latents).transpose(1, 0, 2, 3).reshape(rows, latents)

    def encode(x):
        preact = dot(x, enc) + enc_bias[0]
        feat = jnp.maximum(preact, 0.0) * mask
        return preact, feat, feat.astype(bf16)

    def spread(x):
        same = [x] + [swap(x, 2 * i, count) for i in range(1, chips)]
        return same

    own = x_own.reshape(rows, width)
    preact_own, feat_own, fb_own = encode(own)
    all_own = spread(by_slot(fb_own))
    barred = lax.optimization_barrier((x_far, *all_own))
    x_far, all_own = barred[0], barred[1:]
    far = x_far.reshape(rows, width)
    preact_far, feat_far, fb_far = encode(far)
    all_far = spread(by_slot(fb_far))

    lower = my_half == 0
    same_own, same_far = jnp.stack(all_own), jnp.stack(all_far)
    near_chip = (jnp.arange(chips) < chips // 2)[:, None, None, None]
    flip = jnp.logical_xor(near_chip, lower)
    low = jnp.where(flip, same_far, same_own)
    high = jnp.where(flip, same_own, same_far)
    same = jnp.concatenate([low, high], axis=2)
    span_rows = same.shape[2]
    other = swap(same, 1, count)
    feats_all = jnp.concatenate([same, other]).reshape(count * MOST, span_rows, latents)
    place = (((active % 2) ^ core) * chips + ((active // 2) ^ (me // 2))) * MOST + slot_of

    small = feats_all.size * 4 + dec_all.size * 8 < 40 * 2**20
    r_out, y_out = (decode if small else decode_plain)(
        names, skipped, place.reshape(-1), active.reshape(-1), core.reshape(1), feats_all, dec_all
    )
    y_in = exchange(y_out)
    r_out = r_out.reshape(2, chips, MOST, span_rows, latents)
    r_near = swap(r_out[1], 1, count)
    r_sum = (r_out[0].astype(f32) + r_near.astype(f32)).astype(bf16)
    recon_part = r_sum[0].astype(f32)
    for i in range(1, chips):
        recon_part = recon_part + swap(r_sum[i], 2 * i, count).astype(f32)

    weights = dec.astype(f32)
    base_norm = jnp.sqrt(jnp.sum(weights[:, :stream] * weights[:, :stream], axis=1) + epsilon)
    chat_norm = jnp.sqrt(jnp.sum(weights[:, stream:] * weights[:, stream:], axis=1) + epsilon)
    bias_dec = jnp.sum(weights * dec_bias[None, :], axis=1)
    constant = grad_scale * bias_dec + penalty_weight * (base_norm + chat_norm)
    cross = functools.partial(
        lax.dot_general, dimension_numbers=(((1,), (1,)), ((), ())), preferred_element_type=f32
    )
    xd_own = cross(own, dec)
    xd_far = cross(far, dec)
    down = functools.partial(
        lax.dot_general, dimension_numbers=(((0,), (0,)), ((), ())), preferred_element_type=f32
    )
    fx = down(fb_own, own) + down(fb_far, far)
    feature_sum = jnp.sum(feat_own, axis=0) + jnp.sum(feat_far, axis=0)
    rounded_sum = jnp.sum(fb_own.astype(f32), axis=0) + jnp.sum(fb_far.astype(f32), axis=0)
    inverse = jnp.concatenate(
        [
            jnp.broadcast_to(1.0 / base_norm[:, None], (latents, stream)),
            jnp.broadcast_to(1.0 / chat_norm[:, None], (latents, stream)),
        ],
        axis=1,
    )
    dec_part = (
        grad_scale * (rounded_sum[:, None] * dec_bias[None, :] - fx)
        + penalty_weight * feature_sum[:, None] * weights * inverse
    )

    first, second = recon_part[:, : span_rows // 2], recon_part[:, span_rows // 2 :]
    r_own = by_source(jnp.where(lower, first, second))
    r_far = by_source(jnp.where(lower, second, first))
    grad_own = jnp.where((preact_own > 0.0) & (mask > 0.0), r_own - grad_scale * xd_own + constant, 0.0)
    grad_far = jnp.where((preact_far > 0.0) & (mask > 0.0), r_far - grad_scale * xd_far + constant, 0.0)
    bias_grad = jnp.sum(grad_own, axis=0) + jnp.sum(grad_far, axis=0)
    gb_own, gb_far = grad_own.astype(bf16), grad_far.astype(bf16)

    act_sum = jnp.sum(activations.astype(f32), axis=(0, 1))
    bias_sum = jnp.sum(rounded_sum[:, None] * weights, axis=0) - act_sum
    bias_sum, recon_part = lax.optimization_barrier((bias_sum, recon_part))
    distance = 1
    while distance < count:
        if distance == count // 2:
            bias_sum, gb_own, gb_far = lax.optimization_barrier((bias_sum, gb_own, gb_far))
        bias_sum = bias_sum + swap(bias_sum, distance, count)
        distance *= 2
    dec_bias_grad = grad_scale * (bias_sum + float(span_count * part_rows * count) * dec_bias)
    enc_grad = down(own, gb_own) + down(far, gb_far)
    dec_grad = join_windows(dec_part, y_in, skipped)

    return (enc_grad[None], bias_grad[None], dec_grad[None], dec_bias_grad)


def solution(mesh):
    in_specs = (
        P("group", "latent", None),
        P(("group", "latent"), None, None),
        P(("group", "latent"), None),
        P(("group", "latent"), None, None),
        P("group"),
        P("group", None),
    )
    out_specs = (
        P(("group", "latent"), None, None),
        P(("group", "latent"), None),
        P(("group", "latent"), None, None),
        P("group"),
    )
    return jax.shard_map(shards, mesh=mesh, in_specs=in_specs, out_specs=out_specs, check_vma=False)
```

```python
import functools

import jax
import jax.numpy as jnp
from jax import lax
from jax.experimental import pallas as pl
from jax.experimental.pallas import tpu as pltpu
from jax.sharding import PartitionSpec as P

MOST = 2
AXIS = "latent"

penalty_weight = 0.1
grad_scale = 0.0625
epsilon = 1e-06

f32 = jnp.float32
bf16 = jnp.bfloat16


def swap(x, distance, count):
    return lax.ppermute(x, AXIS, [(i, i ^ distance) for i in range(count)])


def exchange(x, groups=None):
    return lax.all_to_all(
        x, AXIS, split_axis=0, concat_axis=0, tiled=True, axis_index_groups=groups
    )


def slot_tables(active, count):
    blocks = jnp.arange(count, dtype=jnp.int32)
    member = jnp.any(active[:, :, None] == blocks[None, None, :], axis=1).astype(jnp.int32)
    position = jnp.cumsum(member, axis=0) - member
    slots = jnp.arange(MOST, dtype=jnp.int32)
    chosen = member[:, :, None] * (position[:, :, None] == slots).astype(jnp.int32)
    spans = jnp.arange(active.shape[0], dtype=jnp.int32)
    span_of = jnp.sum(chosen * spans[:, None, None], axis=0)
    live = jnp.sum(chosen, axis=0)
    named = active[:, :, None] == blocks[None, None, :]
    slot_of = jnp.sum(jnp.where(named, position[:, None, :], 0), axis=2)
    return span_of, live, slot_of


def pick_kernel(index_ref, rows_ref, out_ref, sems):
    picked = out_ref.shape[0]

    def start(i, carry):
        pltpu.make_async_copy(rows_ref.at[index_ref[i]], out_ref.at[i], sems.at[i]).start()
        return carry

    def wait(i, carry):
        pltpu.make_async_copy(rows_ref.at[0], out_ref.at[i], sems.at[i]).wait()
        return carry

    lax.fori_loop(0, picked, start, 0)
    lax.fori_loop(0, picked, wait, 0)


def pick_spans(rows, index):
    shape = (index.shape[0],) + rows.shape[1:]
    return pl.pallas_call(
        pick_kernel,
        in_specs=[
            pl.BlockSpec(memory_space=pltpu.SMEM),
            pl.BlockSpec(memory_space=pltpu.VMEM),
        ],
        out_specs=pl.BlockSpec(memory_space=pl.ANY),
        out_shape=jax.ShapeDtypeStruct(shape, rows.dtype),
        scratch_shapes=[pltpu.SemaphoreType.DMA((shape[0],))],
        compiler_params=pltpu.CompilerParams(vmem_limit_bytes=48 * 2**20),
        cost_estimate=pl.CostEstimate(flops=0, bytes_accessed=6 * rows.size, transcendentals=0),
        name="pick_spans",
    )(index, rows)


def deal_kernel(index_ref, rows_ref, *refs):
    outs, sems = refs[:-1], refs[-1]
    copies = [
        pltpu.make_async_copy(rows_ref.at[index_ref[i * MOST + slot]], out.at[slot], sems.at[i, slot])
        for i, out in enumerate(outs)
        for slot in range(MOST)
    ]
    for copy in copies:
        copy.start()
    for copy in copies:
        copy.wait()


def deal_spans(rows, index):
    parts = index.shape[0] // MOST
    vmem = pl.BlockSpec(memory_space=pltpu.VMEM)
    return pl.pallas_call(
        deal_kernel,
        in_specs=[pl.BlockSpec(memory_space=pltpu.SMEM), vmem],
        out_specs=[vmem] * parts,
        out_shape=[jax.ShapeDtypeStruct((MOST,) + rows.shape[1:], rows.dtype)] * parts,
        scratch_shapes=[pltpu.SemaphoreType.DMA((parts, MOST))],
        compiler_params=pltpu.CompilerParams(vmem_limit_bytes=48 * 2**20),
        cost_estimate=pl.CostEstimate(flops=0, bytes_accessed=6 * rows.size, transcendentals=0),
        name="deal_spans",
    )(index, rows)


def gather_kernel(place_ref, *refs):
    parts, out_ref, sems = refs[:-2], refs[-2], refs[-1]
    copies = [
        pltpu.make_async_copy(part, out_ref.at[i ^ place_ref[0]], sems.at[i])
        for i, part in enumerate(parts)
    ]
    for copy in copies:
        copy.start()
    for copy in copies:
        copy.wait()


def gather_rows(parts, place):
    count = len(parts)
    return pl.pallas_call(
        gather_kernel,
        in_specs=[pl.BlockSpec(memory_space=pltpu.SMEM)]
        + [pl.BlockSpec(memory_space=pltpu.VMEM)] * count,
        out_specs=pl.BlockSpec(memory_space=pl.ANY),
        out_shape=jax.ShapeDtypeStruct((count,) + parts[0].shape, parts[0].dtype),
        scratch_shapes=[pltpu.SemaphoreType.DMA((count,))],
        compiler_params=pltpu.CompilerParams(vmem_limit_bytes=48 * 2**20),
        cost_estimate=pl.CostEstimate(
            flops=0, bytes_accessed=4 * count * parts[0].size, transcendentals=0
        ),
        name="gather_rows",
    )(place, *parts)


def window_kernel(starts, dec_ref, out_ref, sems):
    width = out_ref.shape[-1]
    copies = [
        pltpu.make_async_copy(dec_ref.at[:, pl.ds(s, width)], out_ref.at[i], sems.at[i])
        for i, s in enumerate(starts)
    ]
    for copy in copies:
        copy.start()
    for copy in copies:
        copy.wait()


def cut_windows(dec, starts, window):
    if any(s % 128 for s in starts) or window % 128:
        return jnp.stack([dec[:, s : s + window] for s in starts])
    return pl.pallas_call(
        functools.partial(window_kernel, starts),
        in_specs=[pl.BlockSpec(memory_space=pltpu.VMEM)],
        out_specs=pl.BlockSpec(memory_space=pl.ANY),
        out_shape=jax.ShapeDtypeStruct((len(starts), dec.shape[0], window), dec.dtype),
        scratch_shapes=[pltpu.SemaphoreType.DMA((len(starts),))],
        cost_estimate=pl.CostEstimate(flops=0, bytes_accessed=4 * dec.size, transcendentals=0),
        name="cut_windows",
    )(dec)


def join_kernel(skipped, part_ref, y_ref, out_ref):
    window = y_ref.shape[-1]
    out_ref[:, :window] = part_ref[:, :window] + y_ref[0].astype(f32)
    out_ref[:, window:] = part_ref[:, window:] + y_ref[1][:, skipped:].astype(f32)


def join_windows(part, y, skipped):
    count, latents, window = y.shape
    if window % 128 or skipped % 128:
        cols = [y[i] if i % 2 == 0 else y[i][:, skipped:] for i in range(count)]
        return part + jnp.concatenate(cols, axis=1).astype(f32)
    per_chip = 2 * window - skipped
    return pl.pallas_call(
        functools.partial(join_kernel, skipped),
        grid=(count // 2,),
        in_specs=[
            pl.BlockSpec((latents, per_chip), lambda i: (0, i)),
            pl.BlockSpec((2, latents, window), lambda i: (i, 0, 0)),
        ],
        out_specs=pl.BlockSpec((latents, per_chip), lambda i: (0, i)),
        out_shape=jax.ShapeDtypeStruct(part.shape, f32),
        name="join_windows",
    )(part, y)


def decode_kernel(names, skipped, place_ref, land_ref, block_ref, mine_ref, *refs):
    own_refs, far_refs, dec_ref, r_ref, y_ref, total, feats, decs = refs[:2], refs[2:4], *refs[4:]
    span_count = place_ref.shape[0] // names
    chips, most, rows, latents = own_refs[0].shape
    r_ref[...] = jnp.zeros_like(r_ref)
    total[...] = jnp.zeros_like(total)

    def span_step(span, carry):
        at = [place_ref[span * names + name] for name in range(names)]
        block = [block_ref[span * names + name] for name in range(names)]
        for name in range(names):
            cols = slice(name * latents, (name + 1) * latents)
            slot = at[name] % most
            chip = at[name] // most % chips
            lower = (chip < chips // 2) == (mine_ref[1] == 0)
            first = pl.multiple_of(jnp.where(lower, 0, rows), rows)
            for core in range(2):

                @pl.when(at[name] // (most * chips) == core)
                def _():
                    feats[pl.ds(first, rows), cols] = own_refs[core][chip, slot]
                    feats[pl.ds(rows - first, rows), cols] = far_refs[core][chip, slot]

            decs[cols, :] = dec_ref[block[name]]
        scaled = jnp.dot(feats[...], decs[...], preferred_element_type=f32) * grad_scale
        if skipped:
            lane = lax.broadcasted_iota(jnp.int32, scaled.shape, 1)
            scaled = jnp.where(lane >= mine_ref[0] * skipped, scaled, 0.0)
        delta = scaled.astype(bf16)
        part = lax.dot_general(
            delta, decs[...], (((1,), (1,)), ((), ())), preferred_element_type=f32
        ).astype(bf16)
        grad = lax.dot_general(
            feats[...], delta, (((0,), (0,)), ((), ())), preferred_element_type=f32
        )
        for name in range(names):
            r_ref[land_ref[span * names + name]] = part[:, name * latents : (name + 1) * latents]
            total[block[name]] += grad[name * latents : (name + 1) * latents]
        return carry

    lax.fori_loop(0, span_count, span_step, 0)
    y_ref[...] = total[...].astype(bf16)


def decode(names, skipped, place, land, block, mine, own, far, dec):
    vmem = pl.BlockSpec(memory_space=pltpu.VMEM)
    smem = pl.BlockSpec(memory_space=pltpu.SMEM)
    pairs, columns = place.shape[0], dec.shape[2]
    chips, most, rows, latents = own[0].shape
    return pl.pallas_call(
        functools.partial(decode_kernel, names, skipped),
        in_specs=[smem] * 4 + [vmem] * 5,
        out_specs=[vmem, vmem],
        out_shape=[
            jax.ShapeDtypeStruct((2 * chips * most, 2 * rows, latents), bf16),
            jax.ShapeDtypeStruct(dec.shape, bf16),
        ],
        scratch_shapes=[
            pltpu.VMEM(dec.shape, f32),
            pltpu.VMEM((2 * rows, names * latents), bf16),
            pltpu.VMEM((names * latents, columns), bf16),
        ],
        compiler_params=pltpu.CompilerParams(vmem_limit_bytes=56 * 2**20),
        cost_estimate=pl.CostEstimate(
            flops=12 * pairs * rows * latents * columns,
            bytes_accessed=4 * (8 * own[0].size + dec.size),
            transcendentals=0,
        ),
        name="decode",
    )(place, land, block, mine, *own, *far, dec)


def decode_plain(names, skipped, place, land, block, mine, own, far, dec):
    span_count = place.shape[0] // names
    chips, most, rows, latents = own[0].shape
    lower = ((jnp.arange(chips) < chips // 2) == (mine[1] == 0))[:, None, None, None]
    feats = jnp.concatenate(
        [
            jnp.concatenate([jnp.where(lower, a, b), jnp.where(lower, b, a)], axis=2)
            for a, b in zip(own, far)
        ]
    ).reshape(-1, 2 * rows, latents)
    r_out = jnp.zeros(feats.shape, bf16)
    total = jnp.zeros(dec.shape, f32)
    width = dec.shape[-1]
    keep = (jnp.arange(width) >= mine[0] * skipped).astype(f32)

    def span_step(span, carry):
        r_out, total = carry
        at = lax.dynamic_slice(place, (span * names,), (names,))
        which = lax.dynamic_slice(block, (span * names,), (names,))
        feat, mine = feats[at], dec[which]
        contrib = jnp.einsum("krl,klc->krc", feat, mine, preferred_element_type=f32).astype(bf16)
        recon = jnp.sum(contrib.astype(f32), axis=0)
        delta = (recon * grad_scale * keep).astype(bf16)
        part = jnp.einsum("rc,klc->krl", delta, mine, preferred_element_type=f32)
        grad = jnp.einsum("krl,rc->klc", feat, delta, preferred_element_type=f32)
        to = lax.dynamic_slice(land, (span * names,), (names,))
        return r_out.at[to].set(part.astype(bf16)), total.at[which].add(grad)

    r_out, total = lax.fori_loop(0, span_count, span_step, (r_out, total))
    return r_out, total.astype(bf16)


def shards(activations, enc_weight, enc_bias, dec_weight, dec_bias, active):
    count = lax.axis_size(AXIS)
    me = lax.axis_index(AXIS)
    span_count, part_rows, width = activations.shape
    names = active.shape[1]
    latents = enc_weight.shape[-1]
    stream = width // 2
    half, chips = count // 2, count // 2
    halves = [[h * half + i for i in range(half)] for h in range(2)]
    same_core = [[2 * i + c for i in range(chips)] for c in range(2)]
    my_half, core = me // half, me % 2
    enc, dec = enc_weight[0], dec_weight[0]
    span_of, live, slot_of = slot_tables(active, count)

    per_chip = width // chips
    if per_chip % 128 == 0:
        window = -(-(per_chip // 2) // 128) * 128
    else:
        window = per_chip // 2
    skipped = 2 * window - per_chip
    starts = [(i // 2) * per_chip + (i % 2) * (per_chip - window) for i in range(count)]

    shape = (half, MOST, part_rows)
    mine = lax.dynamic_slice(span_of, (my_half * half, 0), (half, MOST)).reshape(-1)
    across = swap(activations, half, count)
    x_own = exchange(pick_spans(activations, mine).reshape(shape + (width,)), halves)

    rows = half * MOST * part_rows
    dot = functools.partial(jnp.dot, preferred_element_type=f32)
    my_live = lax.dynamic_slice(live, (me, 0), (1, MOST)).astype(f32)
    mask = jnp.broadcast_to(my_live[0][None, :, None, None], shape + (1,)).reshape(rows, 1)

    def by_slot(x):
        return x.reshape(half, MOST, part_rows, latents).transpose(1, 0, 2, 3).reshape(MOST, -1, latents)

    def by_source(x):
        return x.reshape(MOST, half, part_rows, latents).transpose(1, 0, 2, 3).reshape(rows, latents)

    def encode(x):
        preact = dot(x, enc) + enc_bias[0]
        feat = jnp.maximum(preact, 0.0) * mask
        return preact, feat, feat.astype(bf16)

    def spread(x):
        same = [x] + [swap(x, 2 * i, count) for i in range(1, chips)]
        return same

    def to_both(x):
        same = jnp.stack(x)
        return same, swap(same, 1, count)

    own = x_own.reshape(rows, width)
    preact_own, feat_own, fb_own = encode(own)
    all_own = to_both(spread(by_slot(fb_own)))
    across, *all_own = lax.optimization_barrier((across, *all_own))
    theirs = span_of[me ^ jnp.arange(half)].reshape(-1)
    parts = deal_spans(across, theirs)
    dec_all = exchange(cut_windows(dec, starts, window))
    parts = [parts[0]] + [swap(parts[i], i, count) for i in range(1, half)]
    barred = lax.optimization_barrier((dec_all, *parts))
    dec_all, parts = barred[0], barred[1:]
    far = gather_rows(parts, (me % half).reshape(1)).reshape(rows, width)
    preact_far, feat_far, fb_far = encode(far)
    all_far = to_both(spread(by_slot(fb_far)))

    lower = my_half == 0
    span_rows = 2 * half * part_rows
    side = ((active % 2) ^ core) * chips
    place = (side + ((active // 2) ^ (me // 2))) * MOST + slot_of
    land = (side + active // 2) * MOST + slot_of

    weights = dec.astype(f32)
    base_norm = jnp.sqrt(jnp.sum(weights[:, :stream] * weights[:, :stream], axis=1) + epsilon)
    chat_norm = jnp.sqrt(jnp.sum(weights[:, stream:] * weights[:, stream:], axis=1) + epsilon)
    bias_dec = jnp.sum(weights * dec_bias[None, :], axis=1)
    constant = grad_scale * bias_dec + penalty_weight * (base_norm + chat_norm)
    cross = functools.partial(
        lax.dot_general, dimension_numbers=(((1,), (1,)), ((), ())), preferred_element_type=f32
    )
    xd_own = cross(own, dec)
    xd_far = cross(far, dec)
    down = functools.partial(
        lax.dot_general, dimension_numbers=(((0,), (0,)), ((), ())), preferred_element_type=f32
    )
    fx = down(fb_own, own) + down(fb_far, far)
    feature_sum = jnp.sum(feat_own, axis=0) + jnp.sum(feat_far, axis=0)
    rounded_sum = jnp.sum(fb_own.astype(f32), axis=0) + jnp.sum(fb_far.astype(f32), axis=0)
    inverse = jnp.concatenate(
        [
            jnp.broadcast_to(1.0 / base_norm[:, None], (latents, stream)),
            jnp.broadcast_to(1.0 / chat_norm[:, None], (latents, stream)),
        ],
        axis=1,
    )
    dec_part = (
        grad_scale * (rounded_sum[:, None] * dec_bias[None, :] - fx)
        + penalty_weight * feature_sum[:, None] * weights * inverse
    )
    all_far, dec_part, xd_own, xd_far = lax.optimization_barrier((all_far, dec_part, xd_own, xd_far))

    small = 16 * all_own[0].size + dec_all.size * 8 < 40 * 2**20
    r_out, y_out = (decode if small else decode_plain)(
        names,
        skipped,
        place.reshape(-1),
        land.reshape(-1),
        active.reshape(-1),
        jnp.stack([core, my_half]),
        all_own,
        all_far,
        dec_all,
    )
    r_out = r_out.reshape(2, chips, MOST, span_rows, latents)
    r_near = swap(r_out[1], 1, count)
    r_sum = (r_out[0].astype(f32) + r_near.astype(f32)).astype(bf16)
    r_in, y_out = lax.optimization_barrier((exchange(r_sum, same_core), y_out))
    y_in = exchange(y_out)
    recon_part = jnp.sum(r_in.astype(f32), axis=0)

    first, second = recon_part[:, : span_rows // 2], recon_part[:, span_rows // 2 :]
    r_own = by_source(jnp.where(lower, first, second))
    r_far = by_source(jnp.where(lower, second, first))
    grad_own = jnp.where((preact_own > 0.0) & (mask > 0.0), r_own - grad_scale * xd_own + constant, 0.0)
    grad_far = jnp.where((preact_far > 0.0) & (mask > 0.0), r_far - grad_scale * xd_far + constant, 0.0)
    bias_grad = jnp.sum(grad_own, axis=0) + jnp.sum(grad_far, axis=0)
    gb_own, gb_far = grad_own.astype(bf16), grad_far.astype(bf16)

    act_sum = jnp.sum(activations.astype(f32), axis=(0, 1))
    bias_sum = jnp.sum(rounded_sum[:, None] * weights, axis=0) - act_sum
    bias_sum, recon_part = lax.optimization_barrier((bias_sum, recon_part))
    distance = 1
    while distance < count:
        if distance == count // 2:
            bias_sum, gb_own, gb_far = lax.optimization_barrier((bias_sum, gb_own, gb_far))
        bias_sum = bias_sum + swap(bias_sum, distance, count)
        distance *= 2
    dec_bias_grad = grad_scale * (bias_sum + float(span_count * part_rows * count) * dec_bias)
    enc_grad = down(own, gb_own) + down(far, gb_far)
    dec_grad = join_windows(dec_part, y_in, skipped)

    return (enc_grad[None], bias_grad[None], dec_grad[None], dec_bias_grad)


def solution(mesh):
    in_specs = (
        P("group", "latent", None),
        P(("group", "latent"), None, None),
        P(("group", "latent"), None),
        P(("group", "latent"), None, None),
        P("group"),
        P("group", None),
    )
    out_specs = (
        P(("group", "latent"), None, None),
        P(("group", "latent"), None),
        P(("group", "latent"), None, None),
        P("group"),
    )
    return jax.shard_map(shards, mesh=mesh, in_specs=in_specs, out_specs=out_specs, check_vma=False)
```

```python
import functools

import jax
import jax.numpy as jnp
from jax import lax
from jax.experimental import pallas as pl
from jax.experimental.pallas import tpu as pltpu
from jax.sharding import PartitionSpec as P

MOST = 2
UNROLL = 4
AXIS = "latent"

penalty_weight = 0.1
grad_scale = 0.0625
epsilon = 1e-06

f32 = jnp.float32
bf16 = jnp.bfloat16


def swap(x, distance, count):
    return lax.ppermute(x, AXIS, [(i, i ^ distance) for i in range(count)])


def exchange(x, groups=None):
    return lax.all_to_all(
        x, AXIS, split_axis=0, concat_axis=0, tiled=True, axis_index_groups=groups
    )


def slot_tables(active, count):
    blocks = jnp.arange(count, dtype=jnp.int32)
    member = jnp.any(active[:, :, None] == blocks[None, None, :], axis=1).astype(jnp.int32)
    position = jnp.cumsum(member, axis=0) - member
    slots = jnp.arange(MOST, dtype=jnp.int32)
    chosen = member[:, :, None] * (position[:, :, None] == slots).astype(jnp.int32)
    spans = jnp.arange(active.shape[0], dtype=jnp.int32)
    span_of = jnp.sum(chosen * spans[:, None, None], axis=0)
    live = jnp.sum(chosen, axis=0)
    named = active[:, :, None] == blocks[None, None, :]
    slot_of = jnp.sum(jnp.where(named, position[:, None, :], 0), axis=2)
    name_of = jnp.argmax(active[span_of] == blocks[:, None, None], axis=2).astype(jnp.int32)
    return span_of, live, slot_of, name_of


def pick_kernel(index_ref, rows_ref, out_ref):
    def copy(i, carry):
        out_ref[i] = rows_ref[index_ref[i]]
        return carry

    lax.fori_loop(0, out_ref.shape[0], copy, 0)


def pick_spans(rows, index):
    vmem = pl.BlockSpec(memory_space=pltpu.VMEM)
    return pl.pallas_call(
        pick_kernel,
        in_specs=[pl.BlockSpec(memory_space=pltpu.SMEM), vmem],
        out_specs=vmem,
        out_shape=jax.ShapeDtypeStruct(index.shape + rows.shape[1:], rows.dtype),
        compiler_params=pltpu.CompilerParams(vmem_limit_bytes=48 * 2**20),
        cost_estimate=pl.CostEstimate(flops=0, bytes_accessed=6 * rows.size, transcendentals=0),
        name="pick_spans",
    )(index, rows)


def deal_kernel(index_ref, rows_ref, *outs):
    for i, out in enumerate(outs):
        for slot in range(MOST):
            out[slot] = rows_ref[index_ref[i * MOST + slot]]


def deal_spans(rows, index):
    parts = index.shape[0] // MOST
    vmem = pl.BlockSpec(memory_space=pltpu.VMEM)
    return pl.pallas_call(
        deal_kernel,
        in_specs=[pl.BlockSpec(memory_space=pltpu.SMEM), vmem],
        out_specs=[vmem] * parts,
        out_shape=[jax.ShapeDtypeStruct((MOST,) + rows.shape[1:], rows.dtype)] * parts,
        compiler_params=pltpu.CompilerParams(vmem_limit_bytes=48 * 2**20),
        cost_estimate=pl.CostEstimate(flops=0, bytes_accessed=6 * rows.size, transcendentals=0),
        name="deal_spans",
    )(index, rows)


def gather_kernel(place_ref, *refs):
    parts, out_ref, sems = refs[:-2], refs[-2], refs[-1]
    copies = [
        pltpu.make_async_copy(part, out_ref.at[i ^ place_ref[0]], sems.at[i])
        for i, part in enumerate(parts)
    ]
    for copy in copies:
        copy.start()
    for copy in copies:
        copy.wait()


def gather_rows(parts, place):
    count = len(parts)
    return pl.pallas_call(
        gather_kernel,
        in_specs=[pl.BlockSpec(memory_space=pltpu.SMEM)]
        + [pl.BlockSpec(memory_space=pl.ANY)] * count,
        out_specs=pl.BlockSpec(memory_space=pltpu.VMEM),
        out_shape=jax.ShapeDtypeStruct((count,) + parts[0].shape, parts[0].dtype),
        scratch_shapes=[pltpu.SemaphoreType.DMA((count,))],
        compiler_params=pltpu.CompilerParams(vmem_limit_bytes=48 * 2**20),
        cost_estimate=pl.CostEstimate(
            flops=0, bytes_accessed=4 * count * parts[0].size, transcendentals=0
        ),
        name="gather_rows",
    )(place, *parts)


def pack_kernel(*refs):
    for i, part in enumerate(refs[:-1]):
        refs[-1][i] = part[...]


def pack(parts):
    vmem = pl.BlockSpec(memory_space=pltpu.VMEM)
    return pl.pallas_call(
        pack_kernel,
        in_specs=[vmem] * len(parts),
        out_specs=vmem,
        out_shape=jax.ShapeDtypeStruct((len(parts),) + parts[0].shape, parts[0].dtype),
        compiler_params=pltpu.CompilerParams(vmem_limit_bytes=48 * 2**20),
        cost_estimate=pl.CostEstimate(
            flops=0, bytes_accessed=4 * len(parts) * parts[0].size, transcendentals=0
        ),
        name="pack",
    )(*parts)


def window_kernel(starts, dec_ref, out_ref, sems):
    width = out_ref.shape[-1]
    copies = [
        pltpu.make_async_copy(dec_ref.at[:, pl.ds(s, width)], out_ref.at[i], sems.at[i])
        for i, s in enumerate(starts)
    ]
    for copy in copies:
        copy.start()
    for copy in copies:
        copy.wait()


def cut_windows(dec, starts, window):
    if any(s % 128 for s in starts) or window % 128:
        return jnp.stack([dec[:, s : s + window] for s in starts])
    return pl.pallas_call(
        functools.partial(window_kernel, starts),
        in_specs=[pl.BlockSpec(memory_space=pltpu.VMEM)],
        out_specs=pl.BlockSpec(memory_space=pl.ANY),
        out_shape=jax.ShapeDtypeStruct((len(starts), dec.shape[0], window), dec.dtype),
        scratch_shapes=[pltpu.SemaphoreType.DMA((len(starts),))],
        cost_estimate=pl.CostEstimate(flops=0, bytes_accessed=4 * dec.size, transcendentals=0),
        name="cut_windows",
    )(dec)


def join_kernel(skipped, part_ref, y_ref, out_ref, windows, joined, in_sems, out_sems):
    count, _, window = y_ref.shape
    per_chip = 2 * window - skipped
    arriving, leaving = [], []
    for chip in range(count // 2):
        pair = pl.ds(2 * chip, 2)
        arriving.append(pltpu.make_async_copy(y_ref.at[pair], windows.at[pair], in_sems.at[chip]))
        arriving[-1].start()
    for chip in range(count // 2):
        at = chip * per_chip
        arriving[chip].wait()
        joined[chip, :, :window] = part_ref[:, at : at + window] + windows[2 * chip].astype(f32)
        joined[chip, :, window:] = (
            part_ref[:, at + window : at + per_chip]
            + windows[2 * chip + 1][:, skipped:].astype(f32)
        )
        leaving.append(
            pltpu.make_async_copy(
                joined.at[chip], out_ref.at[:, pl.ds(at, per_chip)], out_sems.at[chip]
            )
        )
        leaving[-1].start()
    for copy in leaving:
        copy.wait()


def join_windows(part, y, skipped):
    count, latents, window = y.shape
    if window % 128 or skipped % 128:
        cols = [y[i] if i % 2 == 0 else y[i][:, skipped:] for i in range(count)]
        return part + jnp.concatenate(cols, axis=1).astype(f32)
    vmem = pl.BlockSpec(memory_space=pltpu.VMEM)
    return pl.pallas_call(
        functools.partial(join_kernel, skipped),
        in_specs=[vmem, pl.BlockSpec(memory_space=pl.ANY)],
        out_specs=pl.BlockSpec(memory_space=pl.ANY),
        out_shape=jax.ShapeDtypeStruct(part.shape, f32),
        scratch_shapes=[
            pltpu.VMEM(y.shape, y.dtype),
            pltpu.VMEM((count // 2, latents, 2 * window - skipped), f32),
            pltpu.SemaphoreType.DMA((count // 2,)),
            pltpu.SemaphoreType.DMA((count // 2,)),
        ],
        compiler_params=pltpu.CompilerParams(vmem_limit_bytes=48 * 2**20),
        cost_estimate=pl.CostEstimate(
            flops=part.size, bytes_accessed=8 * part.size, transcendentals=0
        ),
        name="join_windows",
    )(part, y)


def take_feats(place, rows, feat_refs, store):
    chips, most = feat_refs[0].shape[:2]
    slot = place % most
    chip = place // most % chips
    for core in range(2):

        @pl.when(place // (most * chips) == core)
        def _():
            store(
                chip < chips // 2,
                feat_refs[core][chip, slot, : rows // 2],
                feat_refs[core][chip, slot, rows // 2 : rows],
            )


def decode_kernel(names, place_ref, block_ref, same_ref, other_ref, dec_ref, y_ref, total, feats, decs):
    span_count = place_ref.shape[0] // names
    rows, latents = feats.shape[0], same_ref.shape[3]
    total[...] = jnp.zeros_like(total)

    def span_step(span, carry):
        block = [block_ref[span * names + name] for name in range(names)]
        for name in range(names):
            cols = slice(name * latents, (name + 1) * latents)

            def store(same, own, far):
                first = pl.multiple_of(jnp.where(same, 0, rows // 2), rows // 2)
                feats[pl.ds(first, rows // 2), cols] = own
                feats[pl.ds(rows // 2 - first, rows // 2), cols] = far

            take_feats(place_ref[span * names + name], rows, (same_ref, other_ref), store)
            decs[cols, :] = dec_ref[block[name]]
        scaled = jnp.dot(feats[...], decs[...], preferred_element_type=f32) * grad_scale
        grad = lax.dot_general(
            feats[...], scaled.astype(bf16), (((0,), (0,)), ((), ())), preferred_element_type=f32
        )
        for name in range(names):
            total[block[name]] += grad[name * latents : (name + 1) * latents]
        return carry

    lax.fori_loop(0, span_count, span_step, 0, unroll=UNROLL)
    y_ref[...] = total[...].astype(bf16)


def decode(names, rows, place, block, feats, dec):
    vmem = pl.BlockSpec(memory_space=pltpu.VMEM)
    smem = pl.BlockSpec(memory_space=pltpu.SMEM)
    pairs, columns = place.shape[0], dec.shape[2]
    latents = feats[0].shape[3]
    return pl.pallas_call(
        functools.partial(decode_kernel, names),
        in_specs=[smem] * 2 + [vmem] * 3,
        out_specs=vmem,
        out_shape=jax.ShapeDtypeStruct(dec.shape, bf16),
        scratch_shapes=[
            pltpu.VMEM(dec.shape, f32),
            pltpu.VMEM((rows, names * latents), bf16),
            pltpu.VMEM((names * latents, columns), bf16),
        ],
        compiler_params=pltpu.CompilerParams(vmem_limit_bytes=56 * 2**20),
        cost_estimate=pl.CostEstimate(
            flops=4 * pairs * rows * latents * columns,
            bytes_accessed=4 * (feats[0].size + dec.size),
            transcendentals=0,
        ),
        name="decode",
    )(place, block, *feats, dec)


def gram_kernel(names, skipped, land_ref, block_ref, core_ref, dec_ref, out_ref, decs):
    span_count = block_ref.shape[0] // names
    latents = dec_ref.shape[1]
    out_ref[...] = jnp.zeros_like(out_ref)

    def span_step(span, carry):
        for name in range(names):
            decs[name * latents : (name + 1) * latents] = dec_ref[block_ref[span * names + name]]
        kept = decs[...]
        if skipped:
            lane = lax.broadcasted_iota(jnp.int32, kept.shape, 1)
            kept = jnp.where(lane >= core_ref[0] * skipped, kept, jnp.zeros_like(kept))
        part = lax.dot_general(
            decs[...], kept, (((1,), (1,)), ((), ())), preferred_element_type=f32
        ).astype(bf16)
        for name in range(names):
            for other in range(names - 1):
                from_name = (name + 1 + other) % names
                at = land_ref[span * names + name] * (names - 1) + other
                out_ref[at] = part[
                    from_name * latents : (from_name + 1) * latents,
                    name * latents : (name + 1) * latents,
                ]
        return carry

    lax.fori_loop(0, span_count, span_step, 0)


def gram(names, skipped, land, block, core, dec):
    vmem = pl.BlockSpec(memory_space=pltpu.VMEM)
    smem = pl.BlockSpec(memory_space=pltpu.SMEM)
    places, latents = dec.shape[0] * MOST * (names - 1), dec.shape[1]
    return pl.pallas_call(
        functools.partial(gram_kernel, names, skipped),
        in_specs=[smem] * 3 + [vmem],
        out_specs=vmem,
        out_shape=jax.ShapeDtypeStruct((places, latents, latents), bf16),
        scratch_shapes=[pltpu.VMEM((names * latents, dec.shape[2]), bf16)],
        compiler_params=pltpu.CompilerParams(vmem_limit_bytes=56 * 2**20),
        cost_estimate=pl.CostEstimate(
            flops=2 * block.shape[0] * names * latents * latents * dec.shape[2],
            bytes_accessed=2 * (dec.size + places * latents * latents),
            transcendentals=0,
        ),
        name="gram",
    )(land, block, core, dec)


def back_kernel(names, place_ref, same_ref, other_ref, gram_ref, r_own_ref, r_far_ref):
    r_own_ref[...] = jnp.zeros_like(r_own_ref)
    r_far_ref[...] = jnp.zeros_like(r_far_ref)
    rows = 2 * r_own_ref.shape[1]
    for slot in range(r_own_ref.shape[0]):
        for name in range(names):
            weight = gram_ref[slot, name]

            def store(same, own, far):
                own_part = jnp.dot(own, weight, preferred_element_type=f32) * grad_scale
                far_part = jnp.dot(far, weight, preferred_element_type=f32) * grad_scale
                r_own_ref[slot] += jnp.where(same, own_part, far_part)
                r_far_ref[slot] += jnp.where(same, far_part, own_part)

            take_feats(place_ref[slot * names + name], rows, (same_ref, other_ref), store)


def back(names, rows, place, feats, grams):
    vmem = pl.BlockSpec(memory_space=pltpu.VMEM)
    smem = pl.BlockSpec(memory_space=pltpu.SMEM)
    _, most, _, latents = feats[0].shape
    return pl.pallas_call(
        functools.partial(back_kernel, names),
        in_specs=[smem] + [vmem] * 3,
        out_specs=[vmem, vmem],
        out_shape=[jax.ShapeDtypeStruct((most, rows // 2, latents), f32)] * 2,
        compiler_params=pltpu.CompilerParams(vmem_limit_bytes=56 * 2**20),
        cost_estimate=pl.CostEstimate(
            flops=2 * most * names * rows * latents * latents,
            bytes_accessed=8 * most * rows * latents,
            transcendentals=0,
        ),
        name="back",
    )(place, *feats, grams)


def shards(activations, enc_weight, enc_bias, dec_weight, dec_bias, active):
    count = lax.axis_size(AXIS)
    me = lax.axis_index(AXIS)
    span_count, part_rows, width = activations.shape
    names = active.shape[1]
    latents = enc_weight.shape[-1]
    stream = width // 2
    half, chips = count // 2, count // 2
    halves = [[h * half + i for i in range(half)] for h in range(2)]
    same_core = [[2 * i + c for i in range(chips)] for c in range(2)]
    my_half, core = me // half, me % 2
    enc, dec = enc_weight[0], dec_weight[0]
    span_of, live, slot_of, name_of = slot_tables(active, count)

    per_chip = width // chips
    if per_chip % 128 == 0:
        window = -(-(per_chip // 2) // 128) * 128
    else:
        window = per_chip // 2
    skipped = 2 * window - per_chip
    starts = [(i // 2) * per_chip + (i % 2) * (per_chip - window) for i in range(count)]

    shape = (half, MOST, part_rows)
    mine = lax.dynamic_slice(span_of, (my_half * half, 0), (half, MOST)).reshape(-1)
    across = swap(activations, half, count)
    x_own = exchange(pick_spans(activations, mine).reshape(shape + (width,)), halves)
    theirs = span_of[me ^ jnp.arange(half)].reshape(-1)
    parts = deal_spans(across, theirs)
    windows, x_own, dec, parts, act = lax.optimization_barrier(
        (cut_windows(dec, starts, window), x_own, dec, tuple(parts), activations)
    )
    dec_all = exchange(windows)
    parts = [parts[0]] + [swap(parts[i], i, count) for i in range(1, half)]

    rows = half * MOST * part_rows
    dot = functools.partial(jnp.dot, preferred_element_type=f32)
    my_live = lax.dynamic_slice(live, (me, 0), (1, MOST)).astype(f32)
    mask = jnp.broadcast_to(my_live[0][None, :, None, None], shape + (1,)).reshape(rows, 1)

    def by_slot(x):
        return x.reshape(half, MOST, part_rows, latents).transpose(1, 0, 2, 3).reshape(MOST, -1, latents)

    def by_source(x):
        return x.reshape(MOST, half, part_rows, latents).transpose(1, 0, 2, 3).reshape(rows, latents)

    def encode(x):
        preact = dot(x, enc) + enc_bias[0]
        feat = jnp.maximum(preact, 0.0) * mask
        return preact, feat, feat.astype(bf16)

    own = x_own.reshape(rows, width)
    preact_own, feat_own, fb_own = encode(own)

    weights = dec.astype(f32)
    base_norm = jnp.sqrt(jnp.sum(weights[:, :stream] * weights[:, :stream], axis=1) + epsilon)
    chat_norm = jnp.sqrt(jnp.sum(weights[:, stream:] * weights[:, stream:], axis=1) + epsilon)
    bias_dec = jnp.sum(weights * dec_bias[None, :], axis=1)
    constant = grad_scale * bias_dec + penalty_weight * (base_norm + chat_norm)
    inverse = jnp.concatenate(
        [
            jnp.broadcast_to(1.0 / base_norm[:, None], (latents, stream)),
            jnp.broadcast_to(1.0 / chat_norm[:, None], (latents, stream)),
        ],
        axis=1,
    )
    cross = functools.partial(
        lax.dot_general, dimension_numbers=(((1,), (1,)), ((), ())), preferred_element_type=f32
    )
    down = functools.partial(
        lax.dot_general, dimension_numbers=(((0,), (0,)), ((), ())), preferred_element_type=f32
    )
    xd_own = cross(own, dec)
    fx_own = down(fb_own, own)
    gram_self = cross(dec, dec).astype(bf16)
    act_sum = jnp.sum(act.astype(f32), axis=(0, 1))

    side = ((active % 2) ^ core) * chips
    place = (side + ((active // 2) ^ (me // 2))) * MOST + slot_of
    land = (side + active // 2) * MOST + slot_of
    ahead = half - half // 4
    dec_all, *parts[:ahead] = lax.optimization_barrier((dec_all, *parts[:ahead]))
    grams = gram(names, skipped, land.reshape(-1), active.reshape(-1), core.reshape(1), dec_all)
    grams = grams.reshape(2, chips, MOST, names - 1, latents, latents)
    near = swap(grams[1], 1, count)
    near = (grams[0].astype(f32) + near.astype(f32)).astype(bf16)

    near, xd_own, fx_own, constant, gram_self, act_sum, *parts = lax.optimization_barrier(
        (near, xd_own, fx_own, constant, gram_self, act_sum, *parts)
    )
    gram_in = jnp.sum(exchange(near, same_core).astype(f32), axis=0).astype(bf16)
    far = gather_rows(parts, (me % half).reshape(1)).reshape(rows, width)
    preact_far, feat_far, fb_far = encode(far)
    feature_sum = jnp.sum(feat_own, axis=0) + jnp.sum(feat_far, axis=0)
    rounded_sum = jnp.sum(fb_own.astype(f32), axis=0) + jnp.sum(fb_far.astype(f32), axis=0)
    bias_sum = jnp.sum(rounded_sum[:, None] * weights, axis=0) - act_sum
    coarse = lax.reduce_precision(bias_sum, 8, 7)
    fine = (bias_sum - coarse).astype(bf16)
    coarse = coarse.astype(bf16)
    extra = jnp.stack([coarse, fine]).reshape(MOST, -1, latents)
    extra = jnp.pad(extra, ((0, 0), (0, -extra.shape[1] % 16), (0, 0)))
    feats = jnp.concatenate([by_slot(fb_own), by_slot(fb_far), extra], axis=1)
    same = pack([feats] + [swap(feats, 2 * i, count) for i in range(1, chips)])
    feats = (same, swap(same, 1, count))

    behind, _ = lax.optimization_barrier((far, fb_far))
    xd_far = cross(behind, dec)
    fx = fx_own + down(fb_far, behind)
    dec_part = (
        grad_scale * (rounded_sum[:, None] * dec_bias[None, :] - fx)
        + penalty_weight * feature_sum[:, None] * weights * inverse
    )
    feats, gram_in = lax.optimization_barrier((feats, gram_in))
    last = [x[:, :, rows // MOST * 2 : rows // MOST * 2 + width // latents] for x in feats]
    bias_sum = sum(jnp.sum(x.astype(f32), axis=(0, 1)) for x in last).reshape(width)
    dec_bias_grad = grad_scale * (bias_sum + float(span_count * part_rows * count) * dec_bias)

    y_out = decode(names, 2 * half * part_rows, place.reshape(-1), active.reshape(-1), feats, dec_all)
    y_in = exchange(y_out)

    my_spans = lax.dynamic_slice(span_of, (me, 0), (1, MOST))[0]
    my_names = lax.dynamic_slice(name_of, (me, 0), (1, MOST))[0]
    turn = (my_names[:, None] + jnp.arange(names)) % names
    r_own, r_far = back(
        names,
        2 * half * part_rows,
        jnp.take_along_axis(place[my_spans], turn, axis=1).reshape(-1),
        feats,
        jnp.concatenate([jnp.broadcast_to(gram_self, (MOST, 1) + gram_self.shape), gram_in], axis=1),
    )
    r_own, r_far = by_source(r_own), by_source(r_far)

    grad_own = jnp.where((preact_own > 0.0) & (mask > 0.0), r_own - grad_scale * xd_own + constant, 0.0)
    grad_far = jnp.where((preact_far > 0.0) & (mask > 0.0), r_far - grad_scale * xd_far + constant, 0.0)
    bias_grad = jnp.sum(grad_own, axis=0) + jnp.sum(grad_far, axis=0)
    enc_grad = down(own, grad_own.astype(bf16)) + down(far, grad_far.astype(bf16))

    dec_grad = join_windows(dec_part, y_in, skipped)
    return (enc_grad[None], bias_grad[None], dec_grad[None], dec_bias_grad)


def solution(mesh):
    in_specs = (
        P("group", "latent", None),
        P(("group", "latent"), None, None),
        P(("group", "latent"), None),
        P(("group", "latent"), None, None),
        P("group"),
        P("group", None),
    )
    out_specs = (
        P(("group", "latent"), None, None),
        P(("group", "latent"), None),
        P(("group", "latent"), None, None),
        P("group"),
    )
    return jax.shard_map(shards, mesh=mesh, in_specs=in_specs, out_specs=out_specs, check_vma=False)
```

```python
import functools

import jax
import jax.numpy as jnp
from jax import lax
from jax.experimental import pallas as pl
from jax.experimental.pallas import tpu as pltpu
from jax.sharding import PartitionSpec as P

MOST = 2
UNROLL = 4
AXIS = "latent"

penalty_weight = 0.1
grad_scale = 0.0625
epsilon = 1e-06

f32 = jnp.float32
bf16 = jnp.bfloat16


def swap(x, distance, count):
    return lax.ppermute(x, AXIS, [(i, i ^ distance) for i in range(count)])


def exchange(x, groups=None):
    return lax.all_to_all(
        x, AXIS, split_axis=0, concat_axis=0, tiled=True, axis_index_groups=groups
    )


def slot_tables(active, count):
    blocks = jnp.arange(count, dtype=jnp.int32)
    member = jnp.any(active[:, :, None] == blocks[None, None, :], axis=1).astype(jnp.int32)
    position = jnp.cumsum(member, axis=0) - member
    slots = jnp.arange(MOST, dtype=jnp.int32)
    chosen = member[:, :, None] * (position[:, :, None] == slots).astype(jnp.int32)
    spans = jnp.arange(active.shape[0], dtype=jnp.int32)
    span_of = jnp.sum(chosen * spans[:, None, None], axis=0)
    live = jnp.sum(chosen, axis=0)
    named = active[:, :, None] == blocks[None, None, :]
    slot_of = jnp.sum(jnp.where(named, position[:, None, :], 0), axis=2)
    name_of = jnp.argmax(active[span_of] == blocks[:, None, None], axis=2).astype(jnp.int32)
    return span_of, live, slot_of, name_of


def pick_kernel(index_ref, rows_ref, out_ref):
    def copy(i, carry):
        out_ref[i] = rows_ref[index_ref[i]]
        return carry

    lax.fori_loop(0, out_ref.shape[0], copy, 0)


def pick_spans(rows, index):
    vmem = pl.BlockSpec(memory_space=pltpu.VMEM)
    return pl.pallas_call(
        pick_kernel,
        in_specs=[pl.BlockSpec(memory_space=pltpu.SMEM), vmem],
        out_specs=vmem,
        out_shape=jax.ShapeDtypeStruct(index.shape + rows.shape[1:], rows.dtype),
        compiler_params=pltpu.CompilerParams(vmem_limit_bytes=48 * 2**20),
        cost_estimate=pl.CostEstimate(flops=0, bytes_accessed=6 * rows.size, transcendentals=0),
        name="pick_spans",
    )(index, rows)


def deal_kernel(index_ref, rows_ref, *outs):
    for i, out in enumerate(outs):
        for slot in range(MOST):
            out[slot] = rows_ref[index_ref[i * MOST + slot]]


def deal_spans(rows, index):
    parts = index.shape[0] // MOST
    vmem = pl.BlockSpec(memory_space=pltpu.VMEM)
    return pl.pallas_call(
        deal_kernel,
        in_specs=[pl.BlockSpec(memory_space=pltpu.SMEM), vmem],
        out_specs=[vmem] * parts,
        out_shape=[jax.ShapeDtypeStruct((MOST,) + rows.shape[1:], rows.dtype)] * parts,
        compiler_params=pltpu.CompilerParams(vmem_limit_bytes=48 * 2**20),
        cost_estimate=pl.CostEstimate(flops=0, bytes_accessed=5505024, transcendentals=0),
        name="deal_spans",
    )(index, rows)


def gather_kernel(*refs):
    parts, out_ref, sems = refs[:-2], refs[-2], refs[-1]
    copies = [
        pltpu.make_async_copy(part, out_ref.at[i], sems.at[i]) for i, part in enumerate(parts)
    ]
    for copy in copies:
        copy.start()
    for copy in copies:
        copy.wait()


def gather_rows(parts, cost):
    count = len(parts)
    return pl.pallas_call(
        gather_kernel,
        in_specs=[pl.BlockSpec(memory_space=pl.ANY)] * count,
        out_specs=pl.BlockSpec(memory_space=pltpu.VMEM),
        out_shape=jax.ShapeDtypeStruct((count,) + parts[0].shape, parts[0].dtype),
        scratch_shapes=[pltpu.SemaphoreType.DMA((count,))],
        compiler_params=pltpu.CompilerParams(vmem_limit_bytes=48 * 2**20),
        cost_estimate=pl.CostEstimate(flops=0, bytes_accessed=cost, transcendentals=0),
        name="gather_rows",
    )(*parts)


def order_kernel(place_ref, own_ref, *refs):
    fars, extra_ref, out_ref = refs[:-2], refs[-2], refs[-1]
    count, most = own_ref.shape[:2]
    for slot in range(most):
        for i in range(count):
            out_ref[slot, i] = own_ref[i, slot]
        at = 0
        for far in fars:
            for i in range(far.shape[0]):
                out_ref[slot, count + ((at + i) ^ place_ref[0])] = far[i, slot]
            at += far.shape[0]
        for i in range(extra_ref.shape[1]):
            out_ref[slot, 2 * count + i] = extra_ref[slot, i]


def order_rows(place, own, fars, extra):
    vmem = pl.BlockSpec(memory_space=pltpu.VMEM)
    count, most, rows, latents = own.shape
    return pl.pallas_call(
        order_kernel,
        in_specs=[pl.BlockSpec(memory_space=pltpu.SMEM)] + [vmem] * (2 + len(fars)),
        out_specs=vmem,
        out_shape=jax.ShapeDtypeStruct((most, 2 * count + extra.shape[1], rows, latents), own.dtype),
        compiler_params=pltpu.CompilerParams(vmem_limit_bytes=48 * 2**20),
        cost_estimate=pl.CostEstimate(flops=0, bytes_accessed=8 * own.size, transcendentals=0),
        name="order_rows",
    )(place, own, *fars, extra)


def pack_kernel(*refs):
    for i, part in enumerate(refs[:-1]):
        refs[-1][i] = part[...]


def pack(parts):
    vmem = pl.BlockSpec(memory_space=pltpu.VMEM)
    return pl.pallas_call(
        pack_kernel,
        in_specs=[vmem] * len(parts),
        out_specs=vmem,
        out_shape=jax.ShapeDtypeStruct((len(parts),) + parts[0].shape, parts[0].dtype),
        compiler_params=pltpu.CompilerParams(vmem_limit_bytes=48 * 2**20),
        cost_estimate=pl.CostEstimate(
            flops=0, bytes_accessed=4 * len(parts) * parts[0].size, transcendentals=0
        ),
        name="pack",
    )(*parts)


def window_kernel(starts, dec_ref, out_ref, sems):
    width = out_ref.shape[-1]
    copies = [
        pltpu.make_async_copy(dec_ref.at[:, pl.ds(s, width)], out_ref.at[i], sems.at[i])
        for i, s in enumerate(starts)
    ]
    for copy in copies:
        copy.start()
    for copy in copies:
        copy.wait()


def cut_windows(dec, starts, window):
    if any(s % 128 for s in starts) or window % 128:
        return jnp.stack([dec[:, s : s + window] for s in starts])
    return pl.pallas_call(
        functools.partial(window_kernel, starts),
        in_specs=[pl.BlockSpec(memory_space=pltpu.VMEM)],
        out_specs=pl.BlockSpec(memory_space=pl.ANY),
        out_shape=jax.ShapeDtypeStruct((len(starts), dec.shape[0], window), dec.dtype),
        scratch_shapes=[pltpu.SemaphoreType.DMA((len(starts),))],
        cost_estimate=pl.CostEstimate(flops=0, bytes_accessed=0, transcendentals=0),
        name="cut_windows",
    )(dec)


def join_kernel(window, skipped, part_ref, y_ref, out_ref, windows, joined, in_sems, out_sems):
    count, _, lanes = y_ref.shape
    latents = part_ref.shape[0]
    per_chip = 2 * window - skipped
    arriving, leaving = [], []
    for chip in range(count // 2):
        pair = pl.ds(2 * chip, 2)
        arriving.append(pltpu.make_async_copy(y_ref.at[pair], windows.at[pair], in_sems.at[chip]))
        arriving[-1].start()
    for chip in range(count // 2):
        at = chip * per_chip
        arriving[chip].wait()
        full = (window - skipped) // lanes
        for core in range(2):
            for tile in range(full):
                cols = core * window + tile * lanes
                joined[chip, :, cols : cols + lanes] = part_ref[
                    :, at + cols : at + cols + lanes
                ] + windows[2 * chip + core, tile * latents : (tile + 1) * latents].astype(f32)
            for tile in range(skipped // lanes):
                cols = window - skipped + tile * lanes
                rows = slice(core * latents // 2, (core + 1) * latents // 2)
                first = full * latents + tile * (latents // 2)
                joined[chip, rows, cols : cols + lanes] = part_ref[
                    rows, at + cols : at + cols + lanes
                ] + windows[2 * chip + core, first : first + latents // 2].astype(f32)
        leaving.append(
            pltpu.make_async_copy(
                joined.at[chip], out_ref.at[:, pl.ds(at, per_chip)], out_sems.at[chip]
            )
        )
        leaving[-1].start()
    for copy in leaving:
        copy.wait()


def in_tiles(window, skipped):
    return window % 128 == 0 and skipped % 128 == 0


def join_windows(part, y, window, skipped):
    count, latents = y.shape[0], part.shape[0]
    if not in_tiles(window, skipped):
        cols = [y[i] if i % 2 == 0 else y[i][:, skipped:] for i in range(count)]
        return part + jnp.concatenate(cols, axis=1).astype(f32)
    return pl.pallas_call(
        functools.partial(join_kernel, window, skipped),
        in_specs=[pl.BlockSpec(memory_space=pltpu.VMEM), pl.BlockSpec(memory_space=pl.ANY)],
        out_specs=pl.BlockSpec(memory_space=pl.ANY),
        out_shape=jax.ShapeDtypeStruct(part.shape, f32),
        scratch_shapes=[
            pltpu.VMEM(y.shape, y.dtype),
            pltpu.VMEM((count // 2, latents, 2 * window - skipped), f32),
            pltpu.SemaphoreType.DMA((count // 2,)),
            pltpu.SemaphoreType.DMA((count // 2,)),
        ],
        compiler_params=pltpu.CompilerParams(vmem_limit_bytes=48 * 2**20),
        cost_estimate=pl.CostEstimate(
            flops=part.size, bytes_accessed=8 * part.size, transcendentals=0
        ),
        name="join_windows",
    )(part, y)


def take_feats(place, rows, feat_refs, store):
    chips, most = feat_refs[0].shape[:2]
    slot = place % most
    chip = place // most % chips
    for core in range(2):

        @pl.when(place // (most * chips) == core)
        def _():
            store(
                chip < chips // 2,
                feat_refs[core][chip, slot, : rows // 2],
                feat_refs[core][chip, slot, rows // 2 : rows],
            )


def decode_kernel(names, skipped, place_ref, block_ref, core_ref, same_ref, other_ref, dec_ref, y_ref, total, feats, decs):
    span_count = place_ref.shape[0] // names
    rows, latents = feats.shape[0], same_ref.shape[3]
    total[...] = jnp.zeros_like(total)

    def span_step(span, carry):
        block = [block_ref[span * names + name] for name in range(names)]
        for name in range(names):
            cols = slice(name * latents, (name + 1) * latents)

            def store(same, own, far):
                first = pl.multiple_of(jnp.where(same, 0, rows // 2), rows // 2)
                feats[pl.ds(first, rows // 2), cols] = own
                feats[pl.ds(rows // 2 - first, rows // 2), cols] = far

            take_feats(place_ref[span * names + name], rows, (same_ref, other_ref), store)
            decs[cols, :] = dec_ref[block[name]]
        scaled = jnp.dot(feats[...], decs[...], preferred_element_type=f32) * grad_scale
        grad = lax.dot_general(
            feats[...], scaled.astype(bf16), (((0,), (0,)), ((), ())), preferred_element_type=f32
        )
        for name in range(names):
            total[block[name]] += grad[name * latents : (name + 1) * latents]
        return carry

    lax.fori_loop(0, span_count, span_step, 0, unroll=UNROLL)
    window = decs.shape[1]
    if not in_tiles(window, skipped):
        y_ref[...] = total[...].astype(bf16)
        return
    core, lanes = core_ref[0], y_ref.shape[2]
    full, some = (window - skipped) // lanes, latents // 2
    for tile in range(full):
        cols = pl.ds(pl.multiple_of(core * skipped + tile * lanes, lanes), lanes)
        y_ref[:, tile * latents : (tile + 1) * latents] = total[:, :, cols].astype(bf16)
    for tile in range(skipped // lanes):
        start = jnp.where(core == 0, window - skipped, 0) + tile * lanes
        cols = pl.ds(pl.multiple_of(start, lanes), lanes)
        first = full * latents + tile * some
        y_ref[:, first : first + some] = total[
            :, pl.ds(pl.multiple_of(core * some, some), some), cols
        ].astype(bf16)


def decode(names, skipped, rows, place, block, core, feats, dec):
    vmem = pl.BlockSpec(memory_space=pltpu.VMEM)
    smem = pl.BlockSpec(memory_space=pltpu.SMEM)
    pairs, columns = place.shape[0], dec.shape[2]
    latents = feats[0].shape[3]
    shape = dec.shape
    if in_tiles(columns, skipped):
        shape = (dec.shape[0], (2 * columns - skipped) // 2 * latents // 128, 128)
    return pl.pallas_call(
        functools.partial(decode_kernel, names, skipped),
        in_specs=[smem] * 3 + [vmem] * 3,
        out_specs=vmem,
        out_shape=jax.ShapeDtypeStruct(shape, bf16),
        scratch_shapes=[
            pltpu.VMEM(dec.shape, f32),
            pltpu.VMEM((rows, names * latents), bf16),
            pltpu.VMEM((names * latents, columns), bf16),
        ],
        compiler_params=pltpu.CompilerParams(vmem_limit_bytes=56 * 2**20),
        cost_estimate=pl.CostEstimate(
            flops=4 * pairs * rows * latents * columns,
            bytes_accessed=4 * (feats[0].size + dec.size),
            transcendentals=0,
        ),
        name="decode",
    )(place, block, core, *feats, dec)


def gram_kernel(names, skipped, land_ref, block_ref, core_ref, dec_ref, out_ref, decs):
    span_count = block_ref.shape[0] // names
    latents = dec_ref.shape[1]
    out_ref[...] = jnp.zeros_like(out_ref)

    def span_step(span, carry):
        for name in range(names):
            decs[name * latents : (name + 1) * latents] = dec_ref[block_ref[span * names + name]]
        kept = decs[...]
        if skipped:
            lane = lax.broadcasted_iota(jnp.int32, kept.shape, 1)
            kept = jnp.where(lane >= core_ref[0] * skipped, kept, jnp.zeros_like(kept))
        part = lax.dot_general(
            decs[...], kept, (((1,), (1,)), ((), ())), preferred_element_type=f32
        ).astype(bf16)
        for name in range(names):
            for other in range(names - 1):
                from_name = (name + 1 + other) % names
                at = land_ref[span * names + name] * (names - 1) + other
                out_ref[at] = part[
                    from_name * latents : (from_name + 1) * latents,
                    name * latents : (name + 1) * latents,
                ]
        return carry

    lax.fori_loop(0, span_count, span_step, 0)


def gram(names, skipped, land, block, core, dec):
    vmem = pl.BlockSpec(memory_space=pltpu.VMEM)
    smem = pl.BlockSpec(memory_space=pltpu.SMEM)
    places, latents = dec.shape[0] * MOST * (names - 1), dec.shape[1]
    return pl.pallas_call(
        functools.partial(gram_kernel, names, skipped),
        in_specs=[smem] * 3 + [vmem],
        out_specs=vmem,
        out_shape=jax.ShapeDtypeStruct((places, latents, latents), bf16),
        scratch_shapes=[pltpu.VMEM((names * latents, dec.shape[2]), bf16)],
        compiler_params=pltpu.CompilerParams(vmem_limit_bytes=56 * 2**20),
        cost_estimate=pl.CostEstimate(
            flops=2 * block.shape[0] * names * latents * latents * dec.shape[2],
            bytes_accessed=2 * (dec.size + places * latents * latents),
            transcendentals=0,
        ),
        name="gram",
    )(land, block, core, dec)


def back_kernel(names, place_ref, same_ref, other_ref, gram_ref, r_own_ref, r_far_ref):
    r_own_ref[...] = jnp.zeros_like(r_own_ref)
    r_far_ref[...] = jnp.zeros_like(r_far_ref)
    rows = 2 * r_own_ref.shape[1]
    for slot in range(r_own_ref.shape[0]):
        for name in range(names):
            weight = gram_ref[slot, name]

            def store(same, own, far):
                own_part = jnp.dot(own, weight, preferred_element_type=f32) * grad_scale
                far_part = jnp.dot(far, weight, preferred_element_type=f32) * grad_scale
                r_own_ref[slot] += jnp.where(same, own_part, far_part)
                r_far_ref[slot] += jnp.where(same, far_part, own_part)

            take_feats(place_ref[slot * names + name], rows, (same_ref, other_ref), store)


def back(names, rows, place, feats, grams):
    vmem = pl.BlockSpec(memory_space=pltpu.VMEM)
    smem = pl.BlockSpec(memory_space=pltpu.SMEM)
    _, most, _, latents = feats[0].shape
    return pl.pallas_call(
        functools.partial(back_kernel, names),
        in_specs=[smem] + [vmem] * 3,
        out_specs=[vmem, vmem],
        out_shape=[jax.ShapeDtypeStruct((most, rows // 2, latents), f32)] * 2,
        compiler_params=pltpu.CompilerParams(vmem_limit_bytes=56 * 2**20),
        cost_estimate=pl.CostEstimate(
            flops=2 * most * names * rows * latents * latents,
            bytes_accessed=8 * most * rows * latents,
            transcendentals=0,
        ),
        name="back",
    )(place, *feats, grams)


def shards(activations, enc_weight, enc_bias, dec_weight, dec_bias, active):
    count = lax.axis_size(AXIS)
    me = lax.axis_index(AXIS)
    span_count, part_rows, width = activations.shape
    names = active.shape[1]
    latents = enc_weight.shape[-1]
    stream = width // 2
    half, chips = count // 2, count // 2
    halves = [[h * half + i for i in range(half)] for h in range(2)]
    same_core = [[2 * i + c for i in range(chips)] for c in range(2)]
    my_half, core = me // half, me % 2
    enc, dec = enc_weight[0], dec_weight[0]
    span_of, live, slot_of, name_of = slot_tables(active, count)

    per_chip = width // chips
    if per_chip % 128 == 0:
        window = -(-(per_chip // 2) // 128) * 128
    else:
        window = per_chip // 2
    skipped = 2 * window - per_chip
    starts = [(i // 2) * per_chip + (i % 2) * (per_chip - window) for i in range(count)]

    shape = (half, MOST, part_rows)
    mine = lax.dynamic_slice(span_of, (my_half * half, 0), (half, MOST)).reshape(-1)
    across = swap(activations, half, count)
    x_own = exchange(pick_spans(activations, mine).reshape(shape + (width,)), halves)
    theirs = span_of[me ^ jnp.arange(half)].reshape(-1)
    parts = deal_spans(across, theirs)
    windows, x_own, dec, parts, act = lax.optimization_barrier(
        (cut_windows(dec, starts, window), x_own, dec, tuple(parts), activations)
    )
    dec_all = exchange(windows)
    parts = [parts[0]] + [swap(parts[i], i, count) for i in range(1, half)]

    rows = half * MOST * part_rows
    dot = functools.partial(jnp.dot, preferred_element_type=f32)
    my_live = lax.dynamic_slice(live, (me, 0), (1, MOST)).astype(f32)

    def masked(x):
        parted = x.reshape(-1, MOST, part_rows, latents)
        return jnp.where(my_live[0][None, :, None, None] > 0.0, parted, 0.0).reshape(x.shape)

    def by_source(x):
        return x.reshape(MOST, half, part_rows, latents).transpose(1, 0, 2, 3)

    def encode(x):
        preact = dot(x, enc) + enc_bias[0]
        feat = masked(jnp.maximum(preact, 0.0))
        return preact, feat, feat.astype(bf16)

    own = x_own.reshape(rows, width)
    preact_own, feat_own, fb_own = encode(own)

    weights = dec.astype(f32)
    base_norm = jnp.sqrt(jnp.sum(weights[:, :stream] * weights[:, :stream], axis=1) + epsilon)
    chat_norm = jnp.sqrt(jnp.sum(weights[:, stream:] * weights[:, stream:], axis=1) + epsilon)
    bias_dec = jnp.sum(weights * dec_bias[None, :], axis=1)
    constant = grad_scale * bias_dec + penalty_weight * (base_norm + chat_norm)
    inverse = jnp.concatenate(
        [
            jnp.broadcast_to(1.0 / base_norm[:, None], (latents, stream)),
            jnp.broadcast_to(1.0 / chat_norm[:, None], (latents, stream)),
        ],
        axis=1,
    )
    cross = functools.partial(
        lax.dot_general, dimension_numbers=(((1,), (1,)), ((), ())), preferred_element_type=f32
    )
    down = functools.partial(
        lax.dot_general, dimension_numbers=(((0,), (0,)), ((), ())), preferred_element_type=f32
    )
    xd_own = cross(own, dec)
    fx_own = down(fb_own, own)
    gram_self = cross(dec, dec).astype(bf16)
    act_sum = jnp.sum(act.astype(f32), axis=(0, 1))

    side = ((active % 2) ^ core) * chips
    place = (side + ((active // 2) ^ (me // 2))) * MOST + slot_of
    land = (side + active // 2) * MOST + slot_of
    my_spans = lax.dynamic_slice(span_of, (me, 0), (1, MOST))[0]
    my_names = lax.dynamic_slice(name_of, (me, 0), (1, MOST))[0]
    turn = (my_names[:, None] + jnp.arange(names)) % names
    my_place = jnp.take_along_axis(place[my_spans], turn, axis=1)
    indices = tuple(x.reshape(-1) for x in (place, land, active, my_place, core))
    ahead = half - half // 4
    first_far = gather_rows(parts[:ahead], 1000000).reshape(-1, width)
    dec_all, indices, first_far = lax.optimization_barrier((dec_all, indices, first_far))
    place, land, block, my_place, core_only = indices
    grams = gram(names, skipped, land, block, core_only, dec_all)
    grams = grams.reshape(2, chips, MOST, names - 1, latents, latents)
    near = swap(grams[1], 1, count)
    near = (grams[0].astype(f32) + near.astype(f32)).astype(bf16)

    far = [(first_far, encode(first_far))]
    near, xd_own, fx_own, constant, gram_self, act_sum, far[0], *parts[ahead:] = (
        lax.optimization_barrier(
            (near, xd_own, fx_own, constant, gram_self, act_sum, far[0], *parts[ahead:])
        )
    )
    gram_in = jnp.sum(exchange(near, same_core).astype(f32), axis=0).astype(bf16)
    last_far = gather_rows(parts[ahead:], 0).reshape(-1, width)
    far.append((last_far, encode(last_far)))
    encoded = [(own, (preact_own, feat_own, fb_own))] + far

    feature_sum = sum(jnp.sum(e[1], axis=0) for _, e in encoded)
    rounded_sum = sum(jnp.sum(e[2].astype(f32), axis=0) for _, e in encoded)
    total = lax.reduce_precision(rounded_sum, 8, 7)
    total = jnp.stack([total, rounded_sum - total]).astype(bf16)
    bias_sum = jnp.sum(dot(total, dec), axis=0) - act_sum
    coarse = lax.reduce_precision(bias_sum, 8, 7)
    fine = (bias_sum - coarse).astype(bf16)
    extra = jnp.stack([coarse.astype(bf16), fine]).reshape(MOST, -1, latents)
    extra = jnp.pad(extra, ((0, 0), (0, -extra.shape[1] % part_rows), (0, 0)))
    extra = extra.reshape(MOST, -1, part_rows, latents)
    in_parts = [e[2].reshape(-1, MOST, part_rows, latents) for _, e in encoded]
    feats = order_rows((me % half).reshape(1), in_parts[0], in_parts[1:], extra)
    feats = feats.reshape(MOST, -1, latents)
    over = swap(feats, half, count)
    behind, over = lax.optimization_barrier(([x for x, _ in far], over))
    same = [x if i == 0 else swap(x, 2 * i, count) for x in (feats, over) for i in range(chips // 2)]
    xd_far = [cross(x, dec) for x in behind]
    fx = fx_own + sum(down(e[2], x) for x, (_, e) in zip(behind, far))
    dec_part = (
        grad_scale * (rounded_sum[:, None] * dec_bias[None, :] - fx)
        + penalty_weight * feature_sum[:, None] * weights * inverse
    )
    xd_far, dec_part, *same = lax.optimization_barrier((xd_far, dec_part, *same))
    same = pack(same)
    feats = (same, swap(same, 1, count))

    feats, gram_in = lax.optimization_barrier((feats, gram_in))
    y_out = decode(
        names,
        skipped,
        2 * half * part_rows,
        place,
        block,
        core_only,
        feats,
        dec_all,
    )
    y_in = exchange(y_out)

    r_own, r_far = back(
        names,
        2 * half * part_rows,
        my_place,
        feats,
        jnp.concatenate([jnp.broadcast_to(gram_self, (MOST, 1) + gram_self.shape), gram_in], axis=1),
    )
    r_own, feats = lax.optimization_barrier((r_own, feats))
    last = [x[:, :, rows // MOST * 2 : rows // MOST * 2 + width // latents] for x in feats]
    bias_sum = sum(jnp.sum(x.astype(f32), axis=(0, 1)) for x in last).reshape(width)
    dec_bias_grad = grad_scale * (bias_sum + float(span_count * part_rows * count) * dec_bias)
    r_far = by_source(r_far)[(me % half) ^ jnp.arange(half)]
    r_parts = [by_source(r_own), r_far[:ahead], r_far[ahead:]]

    bias_grad, enc_grad = 0.0, 0.0
    for (x, (preact, _, _)), r, xd in zip(encoded, r_parts, [xd_own] + xd_far):
        grad = r.reshape(preact.shape) - grad_scale * xd + constant
        grad = masked(jnp.where(preact > 0.0, grad, 0.0))
        bias_grad = bias_grad + jnp.sum(grad, axis=0)
        enc_grad = enc_grad + down(x, grad.astype(bf16))

    dec_grad = join_windows(dec_part, y_in, window, skipped)
    return (enc_grad[None], bias_grad[None], dec_grad[None], dec_bias_grad)


def solution(mesh):
    in_specs = (
        P("group", "latent", None),
        P(("group", "latent"), None, None),
        P(("group", "latent"), None),
        P(("group", "latent"), None, None),
        P("group"),
        P("group", None),
    )
    out_specs = (
        P(("group", "latent"), None, None),
        P(("group", "latent"), None),
        P(("group", "latent"), None, None),
        P("group"),
    )
    return jax.shard_map(shards, mesh=mesh, in_specs=in_specs, out_specs=out_specs, check_vma=False)
```

```python
import functools

import jax
import jax.numpy as jnp
from jax import lax
from jax.experimental import pallas as pl
from jax.experimental.pallas import tpu as pltpu
from jax.sharding import PartitionSpec as P

MOST = 2
UNROLL = 4
AXIS = "latent"

penalty_weight = 0.1
grad_scale = 0.0625
epsilon = 1e-06

f32 = jnp.float32
bf16 = jnp.bfloat16


def swap(x, distance, count):
    return lax.ppermute(x, AXIS, [(i, i ^ distance) for i in range(count)])


def exchange(x, groups=None):
    return lax.all_to_all(
        x, AXIS, split_axis=0, concat_axis=0, tiled=True, axis_index_groups=groups
    )


def slot_tables(active, count):
    blocks = jnp.arange(count, dtype=jnp.int32)
    member = jnp.any(active[:, :, None] == blocks[None, None, :], axis=1).astype(jnp.int32)
    position = jnp.cumsum(member, axis=0) - member
    slots = jnp.arange(MOST, dtype=jnp.int32)
    chosen = member[:, :, None] * (position[:, :, None] == slots).astype(jnp.int32)
    spans = jnp.arange(active.shape[0], dtype=jnp.int32)
    span_of = jnp.sum(chosen * spans[:, None, None], axis=0)
    live = jnp.sum(chosen, axis=0)
    named = active[:, :, None] == blocks[None, None, :]
    slot_of = jnp.sum(jnp.where(named, position[:, None, :], 0), axis=2)
    name_of = jnp.argmax(active[span_of] == blocks[:, None, None], axis=2).astype(jnp.int32)
    return span_of, live, slot_of, name_of


def pick_kernel(index_ref, rows_ref, out_ref):
    def copy(i, carry):
        out_ref[i] = rows_ref[index_ref[i]]
        return carry

    lax.fori_loop(0, out_ref.shape[0], copy, 0)


def pick_spans(rows, index):
    vmem = pl.BlockSpec(memory_space=pltpu.VMEM)
    return pl.pallas_call(
        pick_kernel,
        in_specs=[pl.BlockSpec(memory_space=pltpu.SMEM), vmem],
        out_specs=vmem,
        out_shape=jax.ShapeDtypeStruct(index.shape + rows.shape[1:], rows.dtype),
        compiler_params=pltpu.CompilerParams(vmem_limit_bytes=48 * 2**20),
        cost_estimate=pl.CostEstimate(flops=0, bytes_accessed=6 * rows.size, transcendentals=0),
        name="pick_spans",
    )(index, rows)


def deal_kernel(index_ref, rows_ref, *outs):
    for i, out in enumerate(outs):
        for slot in range(MOST):
            out[slot] = rows_ref[index_ref[i * MOST + slot]]


def deal_spans(rows, index):
    parts = index.shape[0] // MOST
    vmem = pl.BlockSpec(memory_space=pltpu.VMEM)
    return pl.pallas_call(
        deal_kernel,
        in_specs=[pl.BlockSpec(memory_space=pltpu.SMEM), vmem],
        out_specs=[vmem] * parts,
        out_shape=[jax.ShapeDtypeStruct((MOST,) + rows.shape[1:], rows.dtype)] * parts,
        compiler_params=pltpu.CompilerParams(vmem_limit_bytes=48 * 2**20),
        cost_estimate=pl.CostEstimate(flops=0, bytes_accessed=5505024, transcendentals=0),
        name="deal_spans",
    )(index, rows)


def gather_kernel(*refs):
    parts, out_ref, sems = refs[:-2], refs[-2], refs[-1]
    copies = [
        pltpu.make_async_copy(part, out_ref.at[i], sems.at[i]) for i, part in enumerate(parts)
    ]
    for copy in copies:
        copy.start()
    for copy in copies:
        copy.wait()


def gather_rows(parts, cost):
    count = len(parts)
    return pl.pallas_call(
        gather_kernel,
        in_specs=[pl.BlockSpec(memory_space=pl.ANY)] * count,
        out_specs=pl.BlockSpec(memory_space=pltpu.VMEM),
        out_shape=jax.ShapeDtypeStruct((count,) + parts[0].shape, parts[0].dtype),
        scratch_shapes=[pltpu.SemaphoreType.DMA((count,))],
        compiler_params=pltpu.CompilerParams(vmem_limit_bytes=48 * 2**20),
        cost_estimate=pl.CostEstimate(flops=0, bytes_accessed=cost, transcendentals=0),
        name="gather_rows",
    )(*parts)


def order_kernel(place_ref, own_ref, *refs):
    fars, extra_ref, out_ref = refs[:-2], refs[-2], refs[-1]
    count, most = own_ref.shape[:2]
    for slot in range(most):
        for i in range(count):
            out_ref[slot, i] = own_ref[i, slot]
        at = 0
        for far in fars:
            for i in range(far.shape[0]):
                out_ref[slot, count + ((at + i) ^ place_ref[0])] = far[i, slot]
            at += far.shape[0]
        for i in range(extra_ref.shape[1]):
            out_ref[slot, 2 * count + i] = extra_ref[slot, i]


def order_rows(place, own, fars, extra):
    vmem = pl.BlockSpec(memory_space=pltpu.VMEM)
    count, most, rows, latents = own.shape
    return pl.pallas_call(
        order_kernel,
        in_specs=[pl.BlockSpec(memory_space=pltpu.SMEM)] + [vmem] * (2 + len(fars)),
        out_specs=vmem,
        out_shape=jax.ShapeDtypeStruct((most, 2 * count + extra.shape[1], rows, latents), own.dtype),
        compiler_params=pltpu.CompilerParams(vmem_limit_bytes=48 * 2**20),
        cost_estimate=pl.CostEstimate(flops=0, bytes_accessed=8 * own.size, transcendentals=0),
        name="order_rows",
    )(place, own, *fars, extra)


def pack_kernel(*refs):
    for i, part in enumerate(refs[:-1]):
        refs[-1][i] = part[...]


def pack(parts):
    vmem = pl.BlockSpec(memory_space=pltpu.VMEM)
    return pl.pallas_call(
        pack_kernel,
        in_specs=[vmem] * len(parts),
        out_specs=vmem,
        out_shape=jax.ShapeDtypeStruct((len(parts),) + parts[0].shape, parts[0].dtype),
        compiler_params=pltpu.CompilerParams(vmem_limit_bytes=48 * 2**20),
        cost_estimate=pl.CostEstimate(
            flops=0, bytes_accessed=4 * len(parts) * parts[0].size, transcendentals=0
        ),
        name="pack",
    )(*parts)


def window_kernel(starts, dec_ref, out_ref, sems):
    width = out_ref.shape[-1]
    copies = [
        pltpu.make_async_copy(dec_ref.at[:, pl.ds(s, width)], out_ref.at[i], sems.at[i])
        for i, s in enumerate(starts)
    ]
    for copy in copies:
        copy.start()
    for copy in copies:
        copy.wait()


def cut_windows(dec, starts, window):
    if any(s % 128 for s in starts) or window % 128:
        return jnp.stack([dec[:, s : s + window] for s in starts])
    return pl.pallas_call(
        functools.partial(window_kernel, starts),
        in_specs=[pl.BlockSpec(memory_space=pltpu.VMEM)],
        out_specs=pl.BlockSpec(memory_space=pl.ANY),
        out_shape=jax.ShapeDtypeStruct((len(starts), dec.shape[0], window), dec.dtype),
        scratch_shapes=[pltpu.SemaphoreType.DMA((len(starts),))],
        cost_estimate=pl.CostEstimate(flops=0, bytes_accessed=0, transcendentals=0),
        name="cut_windows",
    )(dec)


def join_kernel(window, skipped, part_ref, y_ref, out_ref, windows, joined, in_sems, part_sems, out_sems):
    count, _, lanes = y_ref.shape
    latents = part_ref.shape[0]
    per_chip = 2 * window - skipped
    arriving, held, leaving = [], [], []
    for chip in range(count // 2):
        pair = pl.ds(2 * chip, 2)
        arriving.append(pltpu.make_async_copy(y_ref.at[pair], windows.at[pair], in_sems.at[chip]))
        arriving[-1].start()
        cols = pl.ds(chip * per_chip, per_chip)
        held.append(pltpu.make_async_copy(part_ref.at[:, cols], joined.at[chip], part_sems.at[chip]))
        held[-1].start()
    for chip in range(count // 2):
        at = chip * per_chip
        arriving[chip].wait()
        held[chip].wait()
        full = (window - skipped) // lanes
        for core in range(2):
            for tile in range(full):
                cols = core * window + tile * lanes
                joined[chip, :, cols : cols + lanes] += windows[
                    2 * chip + core, tile * latents : (tile + 1) * latents
                ].astype(f32)
            for tile in range(skipped // lanes):
                cols = window - skipped + tile * lanes
                rows = slice(core * latents // 2, (core + 1) * latents // 2)
                first = full * latents + tile * (latents // 2)
                joined[chip, rows, cols : cols + lanes] += windows[
                    2 * chip + core, first : first + latents // 2
                ].astype(f32)
        leaving.append(
            pltpu.make_async_copy(
                joined.at[chip], out_ref.at[:, pl.ds(at, per_chip)], out_sems.at[chip]
            )
        )
        leaving[-1].start()
    for copy in leaving:
        copy.wait()


def in_tiles(window, skipped):
    return window % 128 == 0 and skipped % 128 == 0


def join_windows(part, y, window, skipped):
    count, latents = y.shape[0], part.shape[0]
    if not in_tiles(window, skipped):
        cols = [y[i] if i % 2 == 0 else y[i][:, skipped:] for i in range(count)]
        return part + jnp.concatenate(cols, axis=1).astype(f32)
    return pl.pallas_call(
        functools.partial(join_kernel, window, skipped),
        in_specs=[pl.BlockSpec(memory_space=pltpu.HBM)] * 2,
        out_specs=pl.BlockSpec(memory_space=pl.ANY),
        out_shape=jax.ShapeDtypeStruct(part.shape, f32),
        scratch_shapes=[
            pltpu.VMEM(y.shape, y.dtype),
            pltpu.VMEM((count // 2, latents, 2 * window - skipped), f32),
            pltpu.SemaphoreType.DMA((count // 2,)),
            pltpu.SemaphoreType.DMA((count // 2,)),
            pltpu.SemaphoreType.DMA((count // 2,)),
        ],
        compiler_params=pltpu.CompilerParams(vmem_limit_bytes=48 * 2**20),
        cost_estimate=pl.CostEstimate(
            flops=part.size, bytes_accessed=8 * part.size, transcendentals=0
        ),
        name="join_windows",
    )(part, y)


def take_feats(place, rows, feat_refs, store):
    chips, most = feat_refs[0].shape[:2]
    slot = place % most
    chip = place // most % chips
    for core in range(2):

        @pl.when(place // (most * chips) == core)
        def _():
            store(
                chip < chips // 2,
                feat_refs[core][chip, slot, : rows // 2],
                feat_refs[core][chip, slot, rows // 2 : rows],
            )


def decode_kernel(names, skipped, place_ref, block_ref, core_ref, same_ref, other_ref, dec_ref, y_ref, total, feats, decs):
    span_count = place_ref.shape[0] // names
    rows, latents = feats.shape[0], same_ref.shape[3]
    total[...] = jnp.zeros_like(total)

    def span_step(span, carry):
        block = [block_ref[span * names + name] for name in range(names)]
        for name in range(names):
            cols = slice(name * latents, (name + 1) * latents)

            def store(same, own, far):
                first = pl.multiple_of(jnp.where(same, 0, rows // 2), rows // 2)
                feats[pl.ds(first, rows // 2), cols] = own
                feats[pl.ds(rows // 2 - first, rows // 2), cols] = far

            take_feats(place_ref[span * names + name], rows, (same_ref, other_ref), store)
            decs[cols, :] = dec_ref[block[name]]
        scaled = jnp.dot(feats[...], decs[...], preferred_element_type=f32) * grad_scale
        grad = lax.dot_general(
            feats[...], scaled.astype(bf16), (((0,), (0,)), ((), ())), preferred_element_type=f32
        )
        for name in range(names):
            total[block[name]] += grad[name * latents : (name + 1) * latents]
        return carry

    lax.fori_loop(0, span_count, span_step, 0, unroll=UNROLL)
    window = decs.shape[1]
    if not in_tiles(window, skipped):
        y_ref[...] = total[...].astype(bf16)
        return
    core, lanes = core_ref[0], y_ref.shape[2]
    full, some = (window - skipped) // lanes, latents // 2
    for tile in range(full):
        cols = pl.ds(pl.multiple_of(core * skipped + tile * lanes, lanes), lanes)
        y_ref[:, tile * latents : (tile + 1) * latents] = total[:, :, cols].astype(bf16)
    for tile in range(skipped // lanes):
        start = jnp.where(core == 0, window - skipped, 0) + tile * lanes
        cols = pl.ds(pl.multiple_of(start, lanes), lanes)
        first = full * latents + tile * some
        y_ref[:, first : first + some] = total[
            :, pl.ds(pl.multiple_of(core * some, some), some), cols
        ].astype(bf16)


def decode(names, skipped, rows, place, block, core, feats, dec):
    vmem = pl.BlockSpec(memory_space=pltpu.VMEM)
    smem = pl.BlockSpec(memory_space=pltpu.SMEM)
    pairs, columns = place.shape[0], dec.shape[2]
    latents = feats[0].shape[3]
    shape = dec.shape
    if in_tiles(columns, skipped):
        shape = (dec.shape[0], (2 * columns - skipped) // 2 * latents // 128, 128)
    return pl.pallas_call(
        functools.partial(decode_kernel, names, skipped),
        in_specs=[smem] * 3 + [vmem] * 3,
        out_specs=vmem,
        out_shape=jax.ShapeDtypeStruct(shape, bf16),
        scratch_shapes=[
            pltpu.VMEM(dec.shape, f32),
            pltpu.VMEM((rows, names * latents), bf16),
            pltpu.VMEM((names * latents, columns), bf16),
        ],
        compiler_params=pltpu.CompilerParams(vmem_limit_bytes=56 * 2**20),
        cost_estimate=pl.CostEstimate(
            flops=4 * pairs * rows * latents * columns,
            bytes_accessed=4 * (feats[0].size + dec.size),
            transcendentals=0,
        ),
        name="decode",
    )(place, block, core, *feats, dec)


def gram_kernel(names, skipped, land_ref, block_ref, core_ref, dec_ref, out_ref, decs):
    span_count = block_ref.shape[0] // names
    latents = dec_ref.shape[1]
    out_ref[...] = jnp.zeros_like(out_ref)

    def span_step(span, carry):
        for name in range(names):
            decs[name * latents : (name + 1) * latents] = dec_ref[block_ref[span * names + name]]
        kept = decs[...]
        if skipped:
            lane = lax.broadcasted_iota(jnp.int32, kept.shape, 1)
            kept = jnp.where(lane >= core_ref[0] * skipped, kept, jnp.zeros_like(kept))
        part = lax.dot_general(
            decs[...], kept, (((1,), (1,)), ((), ())), preferred_element_type=f32
        ).astype(bf16)
        for name in range(names):
            for other in range(names - 1):
                from_name = (name + 1 + other) % names
                at = land_ref[span * names + name] * (names - 1) + other
                out_ref[at] = part[
                    from_name * latents : (from_name + 1) * latents,
                    name * latents : (name + 1) * latents,
                ]
        return carry

    lax.fori_loop(0, span_count, span_step, 0, unroll=UNROLL)


def gram(names, skipped, land, block, core, dec):
    vmem = pl.BlockSpec(memory_space=pltpu.VMEM)
    smem = pl.BlockSpec(memory_space=pltpu.SMEM)
    places, latents = dec.shape[0] * MOST * (names - 1), dec.shape[1]
    return pl.pallas_call(
        functools.partial(gram_kernel, names, skipped),
        in_specs=[smem] * 3 + [vmem],
        out_specs=vmem,
        out_shape=jax.ShapeDtypeStruct((places, latents, latents), bf16),
        scratch_shapes=[pltpu.VMEM((names * latents, dec.shape[2]), bf16)],
        compiler_params=pltpu.CompilerParams(vmem_limit_bytes=56 * 2**20),
        cost_estimate=pl.CostEstimate(
            flops=2 * block.shape[0] * names * latents * latents * dec.shape[2],
            bytes_accessed=2 * (dec.size + places * latents * latents),
            transcendentals=0,
        ),
        name="gram",
    )(land, block, core, dec)


def back_kernel(names, place_ref, same_ref, other_ref, self_ref, gram_ref, r_own_ref, r_far_ref):
    r_own_ref[...] = jnp.zeros_like(r_own_ref)
    r_far_ref[...] = jnp.zeros_like(r_far_ref)
    rows = 2 * r_own_ref.shape[1]
    for slot in range(r_own_ref.shape[0]):
        for name in range(names):
            if name == 0:
                weight = self_ref[...]
            else:
                weight = gram_ref[0, slot, name - 1].astype(f32)
                for chip in range(1, gram_ref.shape[0]):
                    weight += gram_ref[chip, slot, name - 1].astype(f32)
                weight = weight.astype(bf16)

            def store(same, own, far):
                own_part = jnp.dot(own, weight, preferred_element_type=f32) * grad_scale
                far_part = jnp.dot(far, weight, preferred_element_type=f32) * grad_scale
                r_own_ref[slot] += jnp.where(same, own_part, far_part)
                r_far_ref[slot] += jnp.where(same, far_part, own_part)

            take_feats(place_ref[slot * names + name], rows, (same_ref, other_ref), store)


def back(names, rows, place, feats, self_gram, grams):
    vmem = pl.BlockSpec(memory_space=pltpu.VMEM)
    smem = pl.BlockSpec(memory_space=pltpu.SMEM)
    _, most, _, latents = feats[0].shape
    return pl.pallas_call(
        functools.partial(back_kernel, names),
        in_specs=[smem] + [vmem] * 4,
        out_specs=[vmem, vmem],
        out_shape=[jax.ShapeDtypeStruct((most, rows // 2, latents), f32)] * 2,
        compiler_params=pltpu.CompilerParams(vmem_limit_bytes=56 * 2**20),
        cost_estimate=pl.CostEstimate(
            flops=2 * most * names * rows * latents * latents,
            bytes_accessed=8 * most * rows * latents,
            transcendentals=0,
        ),
        name="back",
    )(place, *feats, self_gram, grams)


def shards(activations, enc_weight, enc_bias, dec_weight, dec_bias, active):
    count = lax.axis_size(AXIS)
    me = lax.axis_index(AXIS)
    span_count, part_rows, width = activations.shape
    names = active.shape[1]
    latents = enc_weight.shape[-1]
    stream = width // 2
    half, chips = count // 2, count // 2
    halves = [[h * half + i for i in range(half)] for h in range(2)]
    same_core = [[2 * i + c for i in range(chips)] for c in range(2)]
    my_half, core = me // half, me % 2
    enc, dec = enc_weight[0], dec_weight[0]
    span_of, live, slot_of, name_of = slot_tables(active, count)

    per_chip = width // chips
    if per_chip % 128 == 0:
        window = -(-(per_chip // 2) // 128) * 128
    else:
        window = per_chip // 2
    skipped = 2 * window - per_chip
    starts = [(i // 2) * per_chip + (i % 2) * (per_chip - window) for i in range(count)]

    shape = (half, MOST, part_rows)
    mine = lax.dynamic_slice(span_of, (my_half * half, 0), (half, MOST)).reshape(-1)
    across = swap(activations, half, count)
    x_own = exchange(pick_spans(activations, mine).reshape(shape + (width,)), halves)
    theirs = span_of[me ^ jnp.arange(half)].reshape(-1)
    parts = deal_spans(across, theirs)
    windows, x_own, dec, parts, act = lax.optimization_barrier(
        (cut_windows(dec, starts, window), x_own, dec, tuple(parts), activations)
    )
    dec_all = exchange(windows)
    parts = [parts[0]] + [swap(parts[i], i, count) for i in range(1, half)]

    rows = half * MOST * part_rows
    dot = functools.partial(jnp.dot, preferred_element_type=f32)
    my_live = lax.dynamic_slice(live, (me, 0), (1, MOST)).astype(f32)

    def masked(x):
        parted = x.reshape(-1, MOST, part_rows, latents)
        return jnp.where(my_live[0][None, :, None, None] > 0.0, parted, 0.0).reshape(x.shape)

    def by_source(x):
        return x.reshape(MOST, half, part_rows, latents).transpose(1, 0, 2, 3)

    def encode(x):
        preact = dot(x, enc) + enc_bias[0]
        feat = masked(jnp.maximum(preact, 0.0))
        return preact, feat, feat.astype(bf16)

    own = x_own.reshape(rows, width)
    preact_own, feat_own, fb_own = encode(own)

    weights = dec.astype(f32)
    base_norm = jnp.sqrt(jnp.sum(weights[:, :stream] * weights[:, :stream], axis=1) + epsilon)
    chat_norm = jnp.sqrt(jnp.sum(weights[:, stream:] * weights[:, stream:], axis=1) + epsilon)
    bias_dec = jnp.sum(weights * dec_bias[None, :], axis=1)
    constant = grad_scale * bias_dec + penalty_weight * (base_norm + chat_norm)
    inverse = jnp.concatenate(
        [
            jnp.broadcast_to(1.0 / base_norm[:, None], (latents, stream)),
            jnp.broadcast_to(1.0 / chat_norm[:, None], (latents, stream)),
        ],
        axis=1,
    )
    cross = functools.partial(
        lax.dot_general, dimension_numbers=(((1,), (1,)), ((), ())), preferred_element_type=f32
    )
    down = functools.partial(
        lax.dot_general, dimension_numbers=(((0,), (0,)), ((), ())), preferred_element_type=f32
    )
    xd_own = cross(own, dec)
    fx_own = down(fb_own, own)
    gram_self = cross(dec, dec).astype(bf16)
    act_sum = jnp.sum(act.astype(f32), axis=(0, 1))

    side = ((active % 2) ^ core) * chips
    place = (side + ((active // 2) ^ (me // 2))) * MOST + slot_of
    land = (side + active // 2) * MOST + slot_of
    my_spans = lax.dynamic_slice(span_of, (me, 0), (1, MOST))[0]
    my_names = lax.dynamic_slice(name_of, (me, 0), (1, MOST))[0]
    turn = (my_names[:, None] + jnp.arange(names)) % names
    my_place = jnp.take_along_axis(place[my_spans], turn, axis=1)
    indices = tuple(x.reshape(-1) for x in (place, land, active, my_place, core))
    ahead = half * 5 // 8
    first_far = gather_rows(parts[:ahead], 1000000).reshape(-1, width)
    dec_all, indices, first_far = lax.optimization_barrier((dec_all, indices, first_far))
    place, land, block, my_place, core_only = indices
    grams = gram(names, skipped, land, block, core_only, dec_all)
    grams = grams.reshape(2, chips, MOST, names - 1, latents, latents)
    near = swap(grams[1], 1, count)
    near = (grams[0].astype(f32) + near.astype(f32)).astype(bf16)

    far = [(first_far, encode(first_far))]
    near, xd_own, fx_own, constant, gram_self, act_sum, far[0], *parts[ahead:] = (
        lax.optimization_barrier(
            (near, xd_own, fx_own, constant, gram_self, act_sum, far[0], *parts[ahead:])
        )
    )
    gram_in = exchange(near, same_core)
    last_far = gather_rows(parts[ahead:], 0).reshape(-1, width)
    far.append((last_far, encode(last_far)))
    encoded = [(own, (preact_own, feat_own, fb_own))] + far

    feature_sum = sum(jnp.sum(e[1], axis=0) for _, e in encoded)
    rounded_sum = sum(jnp.sum(e[2].astype(f32), axis=0) for _, e in encoded)
    total = lax.reduce_precision(rounded_sum, 8, 7)
    total = jnp.stack([total, rounded_sum - total]).astype(bf16)
    bias_sum = jnp.sum(dot(total, dec), axis=0) - act_sum
    coarse = lax.reduce_precision(bias_sum, 8, 7)
    fine = (bias_sum - coarse).astype(bf16)
    extra = jnp.stack([coarse.astype(bf16), fine]).reshape(MOST, -1, latents)
    extra = jnp.pad(extra, ((0, 0), (0, -extra.shape[1] % part_rows), (0, 0)))
    extra = extra.reshape(MOST, -1, part_rows, latents)
    in_parts = [e[2].reshape(-1, MOST, part_rows, latents) for _, e in encoded]
    feats = order_rows((me % half).reshape(1), in_parts[0], in_parts[1:], extra)
    feats = feats.reshape(MOST, -1, latents)
    over = swap(feats, half, count)
    behind, over = lax.optimization_barrier(([x for x, _ in far], over))
    same = [x if i == 0 else swap(x, 2 * i, count) for x in (feats, over) for i in range(chips // 2)]
    xd_far = [cross(x, dec) for x in behind]
    fx = fx_own + sum(down(e[2], x) for x, (_, e) in zip(behind, far))
    dec_part = (
        grad_scale * (rounded_sum[:, None] * dec_bias[None, :] - fx)
        + penalty_weight * feature_sum[:, None] * weights * inverse
    )
    xd_far, dec_part, *same = lax.optimization_barrier((xd_far, dec_part, *same))
    same = pack(same)
    feats = (same, swap(same, 1, count))

    feats, gram_in = lax.optimization_barrier((feats, gram_in))
    y_out = decode(
        names,
        skipped,
        2 * half * part_rows,
        place,
        block,
        core_only,
        feats,
        dec_all,
    )
    feats, y_out = lax.optimization_barrier((feats, y_out))
    y_in = exchange(y_out)

    r_own, r_far = back(
        names,
        2 * half * part_rows,
        my_place,
        feats,
        gram_self,
        gram_in,
    )
    r_own, feats = lax.optimization_barrier((r_own, feats))
    last = [x[:, :, rows // MOST * 2 : rows // MOST * 2 + width // latents] for x in feats]
    bias_sum = sum(jnp.sum(x.astype(f32), axis=(0, 1)) for x in last).reshape(width)
    dec_bias_grad = grad_scale * (bias_sum + float(span_count * part_rows * count) * dec_bias)
    r_far = by_source(r_far)[(me % half) ^ jnp.arange(half)]
    r_parts = [by_source(r_own), r_far[:ahead], r_far[ahead:]]

    bias_grad, enc_grad = 0.0, 0.0
    for (x, (preact, _, _)), r, xd in zip(encoded, r_parts, [xd_own] + xd_far):
        grad = r.reshape(preact.shape) - grad_scale * xd + constant
        grad = masked(jnp.where(preact > 0.0, grad, 0.0))
        bias_grad = bias_grad + jnp.sum(grad, axis=0)
        enc_grad = enc_grad + down(x, grad.astype(bf16))

    dec_grad = join_windows(dec_part, y_in, window, skipped)
    return (enc_grad[None], bias_grad[None], dec_grad[None], dec_bias_grad)


def solution(mesh):
    in_specs = (
        P("group", "latent", None),
        P(("group", "latent"), None, None),
        P(("group", "latent"), None),
        P(("group", "latent"), None, None),
        P("group"),
        P("group", None),
    )
    out_specs = (
        P(("group", "latent"), None, None),
        P(("group", "latent"), None),
        P(("group", "latent"), None, None),
        P("group"),
    )
    return jax.shard_map(shards, mesh=mesh, in_specs=in_specs, out_specs=out_specs, check_vma=False)
```
